256 devices in a mesh: prefix: 32 (over z, y), sample: 8 (over x, core).
Axes of the slice: x: 4, y: 4, z: 8, core: 2. Of those that a mesh axis runs over, the one named last changes fastest.
Arguments:
- residual: bfloat16 [512, 5376], P(('prefix', 'sample')), may hold values from -6 to 6
- queries: bfloat16 [512, 4096], P(('prefix', 'sample')), may hold values from -133 to 133
- fresh_key_value: bfloat16 [512, 2, 2048], P(('prefix', 'sample')), may hold values from -5 to 5
- prompt_key_value: bfloat16 [16, 2, 4096, 2048], P('sample', None, 'prefix'), may hold values from -5 to 5
- suffix_key_value: bfloat16 [512, 2, 192, 2048], P(('prefix', 'sample')), may hold values from -5 to 5
- suffix_len: int32 [512], P(('prefix', 'sample')), may hold values from 1 to 192, 49152 in all
- sample_prompt: int32 [512], replicated, may hold values from 0 to 15, as said below
- out_weight: bfloat16 [4096, 5376], P('prefix'), may hold values from -0.09375 to 0.09375
- attn_gain: float32 [5376], replicated, may hold values from 0.5 to 1.5
- ffn_gain: float32 [5376], replicated, may hold values from 0.5 to 1.5
- gate_weight: bfloat16 [5376, 21504], P('sample', 'prefix'), may hold values from -0.15625 to 0.15625
- up_weight: bfloat16 [5376, 21504], P('sample', 'prefix'), may hold values from -0.15625 to 0.15625
- down_weight: bfloat16 [21504, 5376], P('prefix', 'sample'), may hold values from -0.078125 to 0.078125
Outputs:
- midway: bfloat16 [512, 5376], P(('prefix', 'sample'))
- ffn_out: bfloat16 [512, 5376], P('prefix', 'sample')
The draws below stay inside these ranges and needn't reach their ends.
Inputs may be any that keep to these rules, and one draw needn't show every extreme that they name: `sample_prompt`: sample s belongs to prompt 2 j or 2 j + 1, with j = (s // 2) % 8; each prompt has exactly 32 samples.
All inputs are finite; a program needn't handle non-finite values. No bound on the sum of `suffix_len` on one device may be relied on, other than what follows from the above.
Results may differ from the reference program's by a relative error of at most 0.025.
Values may be sent and summed in bfloat16 or wider, within the bound.
A program may use at most 64 MiB of HBM per device.

```python
import math
import jax
import jax.numpy as jnp
import numpy as np
from jax import lax

D = 5376
QUERY_HEADS = 32
KEY_VALUE_HEADS = 16
HEAD_WIDTH = 128
FF = 21504
S_DEV = 2
SUFFIX_SLOTS = 192
PROMPT_LENGTH = 4096
PROMPT_COUNT = 16
SAMPLE_COUNT = 512
N_PREFIX = 32
N_SAMPLE = 8


def prompt_keys(key):
    inner_part = jax.random.fold_in(key, 202)
    return jax.random.truncated_normal(inner_part, -4.0, 4.0, (PROMPT_COUNT, PROMPT_LENGTH, KEY_VALUE_HEADS * HEAD_WIDTH), jnp.float32)


def row_ranks(inner_part, rows):
    return jax.random.permutation(inner_part, rows)


def prompt_of(key):
    rows = S_DEV * N_PREFIX
    inner_part = jax.random.split(jax.random.fold_in(key, 101), N_SAMPLE)
    ranks = jax.vmap(partial_rank(rows))(inner_part)
    sample_ids = jnp.arange(SAMPLE_COUNT, dtype=jnp.int32)
    owner = sample_ids // S_DEV
    row_index = owner % N_SAMPLE
    rank_pos = owner // N_SAMPLE * S_DEV + sample_ids % S_DEV
    second = (ranks[row_index, rank_pos] >= rows // 2).astype(jnp.int32)
    return (2 * row_index + second).astype(jnp.int32)


def partial_rank(rows):

    def ranked(inner_part):
        return row_ranks(inner_part, rows)
    return ranked


def draw_sample_prompt(key, part):
    return prompt_of(key)


def draw_prompt_key_value(key, part):
    key_group = prompt_keys(key)
    key = jax.random.fold_in(key, 5)
    value_group = jax.random.truncated_normal(key, -4.0, 4.0, (PROMPT_COUNT, PROMPT_LENGTH, KEY_VALUE_HEADS * HEAD_WIDTH), jnp.float32)
    return jnp.stack([key_group, value_group], axis=1).astype(jnp.bfloat16)


def draw_queries(key, part):
    key = jax.random.fold_in(key, 9)
    values = 2.0 * jax.random.truncated_normal(key, -2.0, 2.0, (SAMPLE_COUNT, QUERY_HEADS * HEAD_WIDTH), jnp.float32)
    return values.astype(jnp.bfloat16)


def spiked(drawn, rng, source, target, parts, factor):
    def block_of(dim):
        return (jnp.arange(drawn.shape[dim]) // (drawn.shape[dim] // parts)).reshape((-1,) + (1,) * (drawn.ndim - 1 - dim))

    first = jax.random.permutation(rng, parts)[block_of(target)]
    far = (block_of(target) + parts // 2) % parts
    return jnp.where((block_of(source) == first) | (block_of(source) == far), factor * drawn, drawn)


def steps_of(rng, extent, cuts, low, high):
    loudness, own = 1.0, jax.random.fold_in(rng, 6)
    for dim, parts in cuts:
        steps = jnp.exp(jax.random.uniform(jax.random.fold_in(own, dim), (parts,), jnp.float32, low / len(cuts), high / len(cuts)))
        loudness = loudness * jnp.repeat(steps, extent[dim] // parts).reshape([-1 if axis == dim else 1 for axis in range(len(extent))])
    return loudness


def length_profile(number_of, total, reach, skew):
    loads = [(1 << 20) // math.isqrt(rank ** skew) + 1 for rank in range(2, number_of + 1)]
    spare, given = total - reach - (number_of - 1), [1] * (number_of - 1)
    while spare > 0:
        candidates = [i for i in range(number_of - 1) if given[i] < reach]
        mass, left = sum([loads[i] for i in candidates]), spare
        for i in candidates:
            more = min(reach - given[i], max(1, left * loads[i] // mass), spare)
            given[i] = given[i] + more
            spare = spare - more
    return np.array([reach] + given)


def ragged(stream_key, number_of, total, most, lean):
    if number_of == 2:
        one = jax.random.randint(stream_key, (), max(1, total - most), min(most, total - 1) + 1)
        return jnp.stack([one, total - one])
    lengths = jnp.asarray(length_profile(number_of, total, most, lean), jnp.int32)
    couples = (number_of - 1) // 2
    giver, taker = lengths[1:1 + 2 * couples:2], lengths[2:2 + 2 * couples:2]
    room = jnp.minimum(giver - 1, most - taker)
    shifted = jax.random.randint(jax.random.fold_in(stream_key, 1), (couples,), 0, 1 << 20) % (room + 1)
    lengths = lengths.at[1:1 + 2 * couples:2].set(giver - shifted).at[2:2 + 2 * couples:2].set(taker + shifted)
    return lengths[jax.random.permutation(jax.random.fold_in(stream_key, 2), number_of)]


def centred(key, extent, deviation, bound, pieces=(), kind=jnp.bfloat16):
    values = deviation * jax.random.normal(key, extent, jnp.float32)
    if pieces:
        values = values * steps_of(key, extent, pieces, -0.22, 0.18)
    return jnp.clip(values, -bound, bound).astype(kind)


def gaussian_with(own_key, shape, scale, limit, pieces, heavy, kind=jnp.bfloat16):
    drawn = scale * jax.random.normal(own_key, shape, jnp.float32)
    if pieces:
        drawn = drawn * steps_of(own_key, shape, pieces, -0.22, 0.18)
    return jnp.clip(spiked(drawn, jax.random.fold_in(own_key, 3), *heavy), -limit, limit).astype(kind)


def setup_inputs(seed: int = 0) -> dict:
    keys = jax.random.split(jax.random.key(seed), 14)
    residual = centred(keys[0], (SAMPLE_COUNT, D), 1.0, 6.0, ((0, 256),))
    queries = draw_queries(jax.random.fold_in(keys[13], 71), 0)
    fresh_key_value = centred(keys[2], (SAMPLE_COUNT, 2, KEY_VALUE_HEADS * HEAD_WIDTH), 1.0, 5.0, ((0, 256),))
    prompt_key_value = draw_prompt_key_value(jax.random.fold_in(keys[13], 71), 0)
    suffix_key_value = centred(keys[4], (SAMPLE_COUNT, 2, SUFFIX_SLOTS, KEY_VALUE_HEADS * HEAD_WIDTH), 1.0, 5.0, ((0, 256),))
    suffix_len = ragged(keys[5], SAMPLE_COUNT, SAMPLE_COUNT * SUFFIX_SLOTS // 2, SUFFIX_SLOTS, 2).astype(jnp.int32)
    sample_prompt = draw_sample_prompt(jax.random.fold_in(keys[13], 71), 0)
    out_weight = centred(keys[7], (QUERY_HEADS * HEAD_WIDTH, D), (QUERY_HEADS * HEAD_WIDTH) ** -0.5, 0.09375, ((0, 32),))
    attn_gain = jnp.clip(1.0 + 0.1 * jax.random.normal(keys[8], (D,), jnp.float32), 0.5, 1.5)
    ffn_gain = jnp.clip(1.0 + 0.1 * jax.random.normal(keys[9], (D,), jnp.float32), 0.5, 1.5)
    gate_weight = gaussian_with(keys[10], (D, FF), D ** -0.5, 0.15625, ((0, 8), (1, 32)), (0, 1, 32, 2.75))
    up_weight = gaussian_with(keys[11], (D, FF), D ** -0.5, 0.15625, ((0, 8), (1, 32)), (0, 1, 32, 2.75))
    down_weight = gaussian_with(keys[12], (FF, D), FF ** -0.5, 0.078125, ((0, 32), (1, 8)), (0, 1, 32, 2.75))
    return {"residual": residual, "queries": queries, "fresh_key_value": fresh_key_value, "prompt_key_value": prompt_key_value, "suffix_key_value": suffix_key_value, "suffix_len": suffix_len, "sample_prompt": sample_prompt, "out_weight": out_weight, "attn_gain": attn_gain, "ffn_gain": ffn_gain, "gate_weight": gate_weight, "up_weight": up_weight, "down_weight": down_weight}


SCALE = 168.0 ** (-0.5)
NEGATIVE = -1e+30
EPSILON = 1e-06

def rms_scale(values, gain_vec):
    mean_square = lax.optimization_barrier(jnp.mean(values * values, axis=-1, keepdims=True))
    return values * lax.rsqrt(mean_square + EPSILON) * gain_vec

def reference(residual, queries, fresh_key_value, prompt_key_value, suffix_key_value, suffix_len, sample_prompt, out_weight, attn_gain, ffn_gain, gate_weight, up_weight, down_weight):
    group_list = QUERY_HEADS // KEY_VALUE_HEADS
    position = jnp.arange(PROMPT_LENGTH + SUFFIX_SLOTS + 1, dtype=jnp.int32)

    def attend(inputs):
        single_query_row, fresh_token, suffix_part, length, prompt_id = inputs
        whole_result = lax.dynamic_index_in_dim(prompt_key_value, prompt_id, 0, keepdims=False)
        key_group = jnp.concatenate([whole_result[0], suffix_part[0], fresh_token[0][None]], axis=0).astype(jnp.float32).reshape(-1, KEY_VALUE_HEADS, HEAD_WIDTH)
        value_group = jnp.concatenate([whole_result[1], suffix_part[1], fresh_token[1][None]], axis=0).astype(jnp.float32).reshape(-1, KEY_VALUE_HEADS, HEAD_WIDTH)
        usable = (position < PROMPT_LENGTH + length) | (position == PROMPT_LENGTH + SUFFIX_SLOTS)
        grouped_rows = single_query_row.astype(jnp.float32).reshape(KEY_VALUE_HEADS, group_list, HEAD_WIDTH)
        logit_scores = jnp.einsum('kgd,nkd->kgn', grouped_rows, key_group) * SCALE
        logit_scores = jnp.where(usable[None, None, :], logit_scores, NEGATIVE)
        row_max = lax.optimization_barrier(jnp.max(logit_scores, axis=-1))
        expo = jnp.exp(logit_scores - row_max[..., None])
        totals = lax.optimization_barrier(jnp.sum(expo, axis=-1))
        weights = lax.optimization_barrier(expo.astype(jnp.bfloat16)).astype(jnp.float32)
        blended = jnp.einsum('kgn,nkd->kgd', weights, value_group) / totals[..., None]
        return blended.reshape(QUERY_HEADS * HEAD_WIDTH).astype(jnp.bfloat16)
    attended = lax.map(attend, (queries, fresh_key_value, suffix_key_value, suffix_len, sample_prompt))
    projected = jnp.dot(attended, out_weight, preferred_element_type=jnp.float32)
    midway = (residual.astype(jnp.float32) + rms_scale(projected, attn_gain)).astype(jnp.bfloat16)
    settled = lax.optimization_barrier(midway).astype(jnp.float32)
    ffn_in = rms_scale(settled, ffn_gain).astype(jnp.bfloat16)
    gate = jnp.dot(ffn_in, gate_weight, preferred_element_type=jnp.float32)
    up_val = jnp.dot(ffn_in, up_weight, preferred_element_type=jnp.float32)
    hidden = (jax.nn.gelu(gate, approximate=True) * up_val).astype(jnp.bfloat16)
    ffn_out = jnp.dot(hidden, down_weight, preferred_element_type=jnp.float32).astype(jnp.bfloat16)
    return (midway, ffn_out)
```

```python
import functools

import jax
import jax.numpy as jnp
from jax import lax
from jax.experimental import pallas as pl
from jax.experimental.pallas import tpu as pltpu
from jax.sharding import PartitionSpec as P

MESH = pl.DeviceIdType.MESH
SCALE = 168.0 ** (-0.5)
NEGATIVE = -1e30
EPSILON = 1e-06
BF = jnp.bfloat16
F32 = jnp.float32

NZ, NY, NX, NC = 8, 4, 4, 2
NP, NS = NZ * NY, NX * NC
HEADS, KV, WIDTH = 32, 16, 128
D = 5376
CHUNKS = D // 128
PROJ_ROWS = 88
BLOCK = 672
SUF = 192
SUFX = 208
Y_OFFSETS = (1, 3, 2)


def dot(a, b):
    return jnp.dot(a, b, preferred_element_type=F32)


def dot_t(a, b):
    return lax.dot_general(a, b, (((1,), (1,)), ((), ())), preferred_element_type=F32)


def remote(src, dst, send_sem, recv_sem, device):
    return pltpu.make_async_remote_copy(
        src_ref=src,
        dst_ref=dst,
        send_sem=send_sem,
        recv_sem=recv_sem,
        device_id=device,
        device_id_type=MESH,
    )


def body(
    q_ref,
    fresh_ref,
    resid_ref,
    again_ref,
    fgain_ref,
    slen_ref,
    sprompt_ref,
    pkv_hbm,
    skv_hbm,
    wout_hbm,
    wg_hbm,
    wu_hbm,
    wd_hbm,
    mid_ref,
    out_ref,
    pkv,
    skv,
    wout,
    wg,
    wu,
    wd,
    load_sem,
    q32,
    qall,
    qflat,
    sel,
    ssuf,
    msufx,
    lsufx,
    osufx,
    stat,
    osend,
    orecv,
    stsend,
    strecv,
    pf,
    psend,
    precv,
    gains,
    resid,
    e1send,
    e1recv,
    e1f,
    xf,
    xall,
    gu,
    gurecv,
    xs,
    xsrecv,
    hid,
    ysend,
    yrecv,
    zsend,
    zrecv,
    aq_z,
    aq_y,
    c_o,
    c_st,
    d_p,
    e_1,
    e_z,
    e_y,
    f_c,
    f_x,
    f_hx,
    f_hc,
    g_y,
    g_z,
):
    me = lax.axis_index("prefix")
    spos = lax.axis_index("sample")
    z, y = me // NY, me % NY
    x, c = spos // NC, spos % NC

    def at_prefix(p):
        return {"prefix": p, "sample": spos}

    def at_zy(zz, yy):
        return {"prefix": zz * NY + yy, "sample": spos}

    def at_sample(s):
        return {"prefix": me, "sample": s}

    def at_xc(xx, cc):
        return {"prefix": me, "sample": xx * NC + cc}

    loads = []

    def load(src, dst):
        cp = pltpu.make_async_copy(src, dst, load_sem.at[len(loads)])
        cp.start()
        loads.append(cp)

    for s in range(2):
        for t in range(2):
            load(skv_hbm.at[s, t], skv.at[s, t, pl.ds(0, SUF)])
    load(pkv_hbm, pkv)
    load(wout_hbm, wout)
    load(wg_hbm, wg)
    load(wu_hbm, wu)
    load(wd_hbm, wd)

    barrier = pltpu.get_barrier_semaphore()

    @pl.loop(1, NP)
    def _(i):
        pl.semaphore_signal(
            barrier, 1, device_id=at_prefix(lax.rem(me + i, NP)), device_id_type=MESH
        )

    @pl.loop(1, NS)
    def _(i):
        pl.semaphore_signal(
            barrier, 1, device_id=at_sample(lax.rem(spos + i, NS)), device_id_type=MESH
        )

    for h in range(HEADS):
        q32[2 * h : 2 * h + 2, :] = q_ref[:, h * 128 : (h + 1) * 128].astype(F32)
    qall[y, z] = q32[...].astype(BF)

    pl.semaphore_wait(barrier, NP - 1 + NS - 1)

    for i in range(1, NZ):
        remote(
            qall.at[y, z],
            qall.at[y, z],
            aq_z.at[0, i],
            aq_z.at[1, z],
            at_zy(lax.rem(z + i, NZ), y),
        ).start()

    @pl.loop(0, 2 * NP)
    def _(r):
        value = sprompt_ref[lax.rem(r, NP) * 16 + 2 * spos + r // NP] - 2 * spos
        row = jnp.full((1, 128), value, jnp.int32).astype(F32)
        sel[pl.ds(r, 1), :] = row
        sel[pl.ds(r + 2 * NP, 1), :] = row

    for j in range(CHUNKS):
        cols = slice(j * 128, (j + 1) * 128)
        resid[2 * j : 2 * j + 2, :] = resid_ref[:, cols].astype(F32)
        gains[0, 2 * j : 2 * j + 2, :] = jnp.broadcast_to(again_ref[:, cols], (2, 128))
        gains[1, 2 * j : 2 * j + 2, :] = jnp.broadcast_to(fgain_ref[:, cols], (2, 128))

    msufx[...] = jnp.full(msufx.shape, NEGATIVE, F32)
    lsufx[...] = jnp.zeros(lsufx.shape, F32)
    osufx[...] = jnp.zeros(osufx.shape, F32)
    first_row = lax.broadcasted_iota(jnp.int32, (16, 2048), 0) == 0
    for s in range(2):
        for t in range(2):
            row = jnp.broadcast_to(fresh_ref[s, t : t + 1, :].astype(F32), (16, 2048))
            skv[s, t, SUF:SUFX, :] = jnp.where(first_row, row, 0.0).astype(BF)
    for s in range(2):
        loads[2 * s].wait()
    for k in range(KV):
        lanes = slice(k * 128, (k + 1) * 128)
        rows = q32[4 * k : 4 * k + 4, :].astype(BF)
        odd = lax.broadcasted_iota(jnp.int32, (4, SUFX), 0) % 2 == 1
        ssuf[4 * k : 4 * k + 4, :] = jnp.where(
            odd, dot_t(rows, skv[1, 0, :, lanes]), dot_t(rows, skv[0, 0, :, lanes])
        )
    odd = lax.broadcasted_iota(jnp.int32, (64, SUFX), 0) % 2 == 1
    slot = lax.broadcasted_iota(jnp.int32, (64, SUFX), 1)
    length = jnp.where(odd, slen_ref[1], slen_ref[0])
    scores = jnp.where((slot < length) | (slot == SUF), ssuf[...] * SCALE, NEGATIVE)
    msuf = jnp.max(scores, axis=1, keepdims=True)
    expo = jnp.exp(scores - msuf)
    lsuf = jnp.broadcast_to(jnp.sum(expo, axis=1, keepdims=True), (64, 128))
    msuf = jnp.broadcast_to(msuf, (64, 128))
    even_w = jnp.where(odd, 0.0, expo)
    odd_w = jnp.where(odd, expo, 0.0)
    for s in range(2):
        loads[2 * s + 1].wait()
    for k in range(KV):
        lanes = slice(k * 128, (k + 1) * 128)
        part = slice(4 * k, 4 * k + 4)
        o = dot(even_w[part].astype(BF), skv[0, 1, :, lanes]) + dot(
            odd_w[part].astype(BF), skv[1, 1, :, lanes]
        )
        for g in range(2):
            for s in range(2):
                src = 4 * k + 2 * g + s
                dst = k * 128 + g * 64 + s * 32 + me
                msufx[pl.ds(dst, 1), :] = msuf[src : src + 1]
                lsufx[pl.ds(dst, 1), :] = lsuf[src : src + 1]
                osufx[pl.ds(dst, 1), :] = o[2 * g + s : 2 * g + s + 1]

    def q_slot(zz):
        return qall.at[y, zz]

    for i in range(1, NZ):
        zz = lax.rem(z + i, NZ)
        remote(q_slot(zz), q_slot(zz), aq_z.at[0, i], aq_z.at[1, zz], at_zy(z, y)).wait_recv()
    for i in Y_OFFSETS:
        remote(
            qall.at[y],
            qall.at[y],
            aq_y.at[0, i],
            aq_y.at[1, y],
            at_zy(z, lax.rem(y + i, NY)),
        ).start()
    for i in range(1, NZ):
        zz = lax.rem(z + i, NZ)
        remote(q_slot(z), q_slot(z), aq_z.at[0, i], aq_z.at[1, zz], at_zy(z, y)).wait_send()

    def widen(yy):
        for zz in range(NZ):
            start = pl.multiple_of((zz * NY + yy) * 64, 64)
            qflat[pl.ds(start, 64), :] = qall[yy, zz].astype(F32)

    widen(y)
    for i in Y_OFFSETS:
        yy = lax.rem(y + i, NY)
        remote(qall.at[yy], qall.at[yy], aq_y.at[0, i], aq_y.at[1, yy], at_zy(z, y)).wait_recv()
        widen(yy)
    for i in Y_OFFSETS:
        remote(qall.at[y], qall.at[y], aq_y.at[0, i], aq_y.at[1, y], at_zy(z, y)).wait_send()

    loads[4].wait()
    chosen = sel[...] > 0.5
    lane = lax.broadcasted_iota(jnp.int32, (128, 128), 1)

    def o_copy(k, g):
        h = 2 * k + g
        return remote(
            osend.at[k, g], orecv.at[me], c_o.at[0, h], c_o.at[1, me], at_prefix(h)
        )

    @pl.loop(0, KV)
    def _(i):
        k = lax.rem(me // 2 + 1 + i, KV)
        lanes = pl.ds(pl.multiple_of(k * 128, 128), 128)
        rows = pl.ds(pl.multiple_of(k * 128, 128), 128)
        q = jnp.concatenate(
            [qflat[pl.ds(4 * k + t, 32, stride=64), :] for t in range(4)], axis=0
        ).astype(BF)
        scores = jnp.where(chosen, dot_t(q, pkv[1, 0, :, lanes]), dot_t(q, pkv[0, 0, :, lanes]))
        scores = scores * SCALE
        ms = msufx[rows, :]
        m = jnp.maximum(ms, jnp.max(scores, axis=1, keepdims=True))
        expo = jnp.exp(scores - m)
        a = jnp.exp(ms - m)
        total = jnp.sum(expo, axis=1, keepdims=True) + a * lsufx[rows, :]
        w0 = jnp.where(chosen, 0.0, expo).astype(BF)
        w1 = jnp.where(chosen, expo, 0.0).astype(BF)
        o = dot(w0, pkv[0, 1, :, lanes]) + dot(w1, pkv[1, 1, :, lanes]) + a * osufx[rows, :]
        o = o.astype(BF)
        stat[...] = jnp.where(lane == k, m, jnp.where(lane == KV + k, total, stat[...]))
        for g in range(2):
            osend[k, g] = o[g * 64 : (g + 1) * 64]

            @pl.when(2 * k + g != me)
            def _():
                o_copy(k, g).start()

            @pl.when(2 * k + g == me)
            def _():
                orecv[me] = o[g * 64 : (g + 1) * 64]

    turned = stat[...].T
    stsend[...] = jnp.zeros(stsend.shape, F32)
    stsend[pl.ds(0, KV, stride=8), :] = turned[0:KV]
    stsend[pl.ds(1, KV, stride=8), :] = turned[KV : 2 * KV]

    def tile(n):
        return pl.ds(pl.multiple_of(n * 8, 8), 8)

    def st_copy(i):
        h = lax.rem(me + i, NP)
        return remote(
            stsend.at[tile(h // 2)],
            strecv.at[tile(me)],
            c_st.at[0, i],
            c_st.at[1, me],
            at_prefix(h),
        )

    @pl.loop(1, NP)
    def _(i):
        st_copy(i).start()

    strecv[tile(me), :] = stsend[tile(me // 2), :]

    @pl.loop(1, NP)
    def _(i):
        src = lax.rem(me + i, NP)
        remote(
            stsend.at[tile(0)], strecv.at[tile(src)], c_st.at[0, i], c_st.at[1, src], at_prefix(me)
        ).wait_recv()
        remote(
            osend.at[0, 0], orecv.at[src], c_o.at[0, src], c_o.at[1, src], at_prefix(me)
        ).wait_recv()

    maxima = strecv[pl.ds(0, NP, stride=8), :]
    totals = strecv[pl.ds(1, NP, stride=8), :]
    second = jnp.zeros((NP, 128), jnp.int32) + lax.rem(me, 2) == 1
    maxima = jnp.where(second, pltpu.roll(maxima, 64, 1), maxima)
    totals = jnp.where(second, pltpu.roll(totals, 64, 1), totals)
    factor = jnp.exp(maxima - jnp.max(maxima, axis=0, keepdims=True))
    share = factor / jnp.sum(factor * totals, axis=0, keepdims=True)
    share = jnp.concatenate([share, jnp.zeros((128 - NP, 128), F32)], axis=0).T[0:64]
    merged = jnp.zeros((64, 128), F32)
    for p in range(NP):
        merged = merged + share[:, p : p + 1] * orecv[p].astype(F32)
    attended = merged.astype(BF)

    loads[5].wait()
    for j in range(CHUNKS // 2):
        r = dot(attended, wout[:, 256 * j : 256 * (j + 1)])
        for t in range(2):
            for s in range(2):
                pf[pl.ds(4 * j + 2 * t + s, NP, stride=PROJ_ROWS), :] = r[
                    s * 32 : (s + 1) * 32, t * 128 : (t + 1) * 128
                ]
    for s in range(2 * CHUNKS, PROJ_ROWS):
        pf[pl.ds(s, NP, stride=PROJ_ROWS), :] = jnp.zeros((NP, 128), F32)

    def narrowed(o):
        return pf[pl.ds(pl.multiple_of(o * PROJ_ROWS, 8), PROJ_ROWS), :].astype(BF)

    def p_copy(i):
        o = lax.rem(me + i, NP)
        return remote(psend.at[o], precv.at[me], d_p.at[0, i], d_p.at[1, me], at_prefix(o))

    @pl.loop(1, NP)
    def _(i):
        o = lax.rem(me + i, NP)
        psend[o] = narrowed(o)
        p_copy(i).start()

    precv[me] = narrowed(me)

    @pl.loop(1, NP)
    def _(i):
        src = lax.rem(me + i, NP)
        remote(
            psend.at[0], precv.at[src], d_p.at[0, i], d_p.at[1, src], at_prefix(me)
        ).wait_recv()

    projected = precv[0].astype(F32)
    for p in range(1, NP):
        projected = projected + precv[p].astype(F32)

    row = lax.broadcasted_iota(jnp.int32, (PROJ_ROWS, 128), 0)
    odd = row % 2 == 1
    real = row < 2 * CHUNKS

    def normed(values, gain):
        square = jnp.where(real, values * values, 0.0)
        second = jnp.sum(jnp.where(odd, square, 0.0))
        first = jnp.sum(jnp.where(odd, 0.0, square))
        inv = jnp.where(odd, second, first) * (1.0 / D) + EPSILON
        return values * lax.rsqrt(inv) * gain

    midway = (resid[...] + normed(projected, gains[0])).astype(BF)
    settled = midway.astype(F32)
    ffn_in = normed(settled, gains[1]).astype(BF).astype(F32)
    ffn_in = jnp.where(real, ffn_in, 0.0)

    lane = lax.broadcasted_iota(jnp.int32, (12, 128), 1)
    rolled = [ffn_in if o == 0 else pltpu.roll(ffn_in, 128 - o, 1) for o in (0, 32, 64, 96)]
    for b in range(NS):
        o, j0 = 32 * (b % 4), (21 * b) // 4
        v = rolled[b % 4]
        piece = v[2 * j0 : 2 * j0 + 12]
        if o:
            piece = jnp.where(lane < 128 - o, piece, v[2 * j0 + 2 : 2 * j0 + 14])
        e1send[b] = jnp.concatenate([piece, jnp.zeros((4, 128), F32)], axis=0).astype(BF)

    def e_copy(i):
        b = lax.rem(spos + i, NS)
        return remote(e1send.at[b], e1recv.at[spos], e_1.at[0, i], e_1.at[1, spos], at_sample(b))

    for i in range(1, NS):
        e_copy(i).start()
    e1recv[spos] = e1send[spos]
    for j in range(CHUNKS):
        mid_ref[:, j * 128 : (j + 1) * 128] = settled[2 * j : 2 * j + 2].astype(BF)
    for i in range(1, NS):
        src = lax.rem(spos + i, NS)
        remote(
            e1send.at[0], e1recv.at[src], e_1.at[0, i], e_1.at[1, src], at_sample(spos)
        ).wait_recv()
    for b in range(NS):
        e1f[16 * b : 16 * (b + 1), :] = e1recv[b].astype(F32)
    for i in range(6):
        for s in range(2):
            xf[i, pl.ds(s, 8, stride=2), :] = e1f[pl.ds(2 * i + s, 8, stride=16), :]
    for i in range(6):
        xall[y, z, :, i * 128 : (i + 1) * 128] = xf[i].astype(BF)

    for i in range(1, NZ):
        remote(
            xall.at[y, z],
            xall.at[y, z],
            e_z.at[0, i],
            e_z.at[1, z],
            at_zy(lax.rem(z + i, NZ), y),
        ).start()
    for i in range(1, NZ):
        zz = lax.rem(z + i, NZ)
        remote(
            xall.at[y, z], xall.at[y, zz], e_z.at[0, i], e_z.at[1, zz], at_zy(z, y)
        ).wait_recv()
    for i in Y_OFFSETS:
        remote(
            xall.at[y], xall.at[y], e_y.at[0, i], e_y.at[1, y], at_zy(z, lax.rem(y + i, NY))
        ).start()

    for n in (6, 7, 8):
        loads[n].wait()
    order = (0,) + Y_OFFSETS
    ending = []

    def in_chunk(ci):
        i = order[ci]
        yy = lax.rem(y + i, NY)
        if i:
            remote(
                xall.at[y], xall.at[yy], e_y.at[0, i], e_y.at[1, yy], at_zy(z, y)
            ).wait_recv()
        v = xall[yy].reshape(128, 768)[:, :BLOCK]
        gu[ci, :, 0] = dot(v, wg[...]).astype(BF).reshape(NZ, 16, BLOCK)
        gu[ci, :, 1] = dot(v, wu[...]).astype(BF).reshape(NZ, 16, BLOCK)
        cp = remote(
            gu.at[ci, pl.ds(4 * (1 - c), 4)],
            gurecv.at[ci],
            f_c.at[0, ci],
            f_c.at[1, ci],
            at_xc(x, 1 - c),
        )
        cp.start()
        return cp

    core_copies = [None] * 4
    hid_copies = [None] * 4
    x_copies = [[] for _ in range(4)]

    def stage_a(ci):
        core_copies[ci] = in_chunk(ci)

    def stage_b(ci):
        core_copies[ci].wait_recv()
        ending.append(core_copies[ci])
        for xx in range(NX):
            xs[ci, xx] = (gu[ci, 4 * c + xx].astype(F32) + gurecv[ci, xx].astype(F32)).astype(BF)
        for i in (1, 3, 2):
            xx = lax.rem(x + i, NX)
            cp = remote(
                xs.at[ci, xx],
                xsrecv.at[ci, i],
                f_x.at[0, ci, i],
                f_x.at[1, ci, i],
                at_xc(xx, c),
            )
            cp.start()
            x_copies[ci].append(cp)

    def stage_c(ci):
        total = xs[ci, x].astype(F32)
        for cp, i in zip(x_copies[ci], (1, 3, 2)):
            cp.wait_recv()
            total = total + xsrecv[ci, i].astype(F32)
        ending.extend(x_copies[ci])
        hidden = (jax.nn.gelu(total[0], approximate=True) * total[1]).astype(BF)
        hid[ci, 4 * c + x] = hidden
        x_copies[ci] = []
        for i in (1, 3, 2):
            cp = remote(
                hid.at[ci, 4 * c + x],
                hid.at[ci, 4 * c + x],
                f_hx.at[0, ci, i],
                f_hx.at[1, ci, x],
                at_xc(lax.rem(x + i, NX), c),
            )
            cp.start()
            ending.append(cp)

    def stage_d(ci):
        for i in (1, 3, 2):
            xx = lax.rem(x + i, NX)
            remote(
                hid.at[ci, 0],
                hid.at[ci, 4 * c + xx],
                f_hx.at[0, ci, i],
                f_hx.at[1, ci, xx],
                at_xc(x, c),
            ).wait_recv()
        half = hid.at[ci, pl.ds(4 * c, 4)]
        cp = remote(half, half, f_hc.at[0, ci], f_hc.at[1, ci], at_xc(x, 1 - c))
        cp.start()
        hid_copies[ci] = cp
        ending.append(cp)

    def stage_e(ci):
        half = hid.at[ci, pl.ds(4 * (1 - c), 4)]
        remote(half, half, f_hc.at[0, ci], f_hc.at[1, ci], at_xc(x, c)).wait_recv()
        i = order[ci]
        ysend[ci] = dot(hid[ci].reshape(128, BLOCK), wd[...]).astype(BF).reshape(NZ, 16, BLOCK)
        if i:
            cp = remote(
                ysend.at[ci],
                yrecv.at[ci],
                g_y.at[0, ci],
                g_y.at[1, ci],
                at_zy(z, lax.rem(y + i, NY)),
            )
            cp.start()
            ending.append(cp)

    stages = (stage_a, stage_b, stage_c, stage_d, stage_e)
    for t in range(4 + 4):
        for st in reversed(range(5)):
            if 0 <= t - st < 4:
                stages[st](t - st)

    for ci in range(1, 4):
        remote(
            ysend.at[ci], yrecv.at[ci], g_y.at[0, ci], g_y.at[1, ci], at_zy(z, y)
        ).wait_recv()
    for zz in range(NZ):
        total = ysend[0, zz].astype(F32)
        for ci in range(1, 4):
            total = total + yrecv[ci, zz].astype(F32)
        zsend[zz] = total.astype(BF)
    for i in range(1, NZ):
        zz = lax.rem(z + i, NZ)
        cp = remote(zsend.at[zz], zrecv.at[i], g_z.at[0, i], g_z.at[1, i], at_zy(zz, y))
        cp.start()
        ending.append(cp)
    total = zsend[z].astype(F32)
    for i in range(1, NZ):
        remote(zsend.at[0], zrecv.at[i], g_z.at[0, i], g_z.at[1, i], at_zy(z, y)).wait_recv()
        total = total + zrecv[i].astype(F32)
    out_ref[...] = total.astype(BF)

    for cp in ending:
        cp.wait_send()

    @pl.loop(0, NP)
    def _(h):
        @pl.when(h != me)
        def _():
            o_copy(h // 2, lax.rem(h, 2)).wait_send()

    @pl.loop(1, NP)
    def _(i):
        st_copy(i).wait_send()
        p_copy(i).wait_send()

    for i in range(1, NS):
        e_copy(i).wait_send()
    for i in range(1, NZ):
        remote(xall.at[y, z], xall.at[y, z], e_z.at[0, i], e_z.at[1, z], at_zy(z, y)).wait_send()
    for i in Y_OFFSETS:
        remote(xall.at[y], xall.at[y], e_y.at[0, i], e_y.at[1, y], at_zy(z, y)).wait_send()


def local(
    residual,
    queries,
    fresh_key_value,
    prompt_key_value,
    suffix_key_value,
    suffix_len,
    sample_prompt,
    out_weight,
    attn_gain,
    ffn_gain,
    gate_weight,
    up_weight,
    down_weight,
):
    vmem = pl.BlockSpec(memory_space=pltpu.VMEM)
    smem = pl.BlockSpec(memory_space=pltpu.SMEM)
    hbm = pl.BlockSpec(memory_space=pl.ANY)
    V = pltpu.VMEM
    dma = pltpu.SemaphoreType.DMA
    scratch = [
        V((2, 2, 128, 2048), BF),
        V((2, 2, SUFX, 2048), BF),
        V((128, D), BF),
        V((BLOCK, BLOCK), BF),
        V((BLOCK, BLOCK), BF),
        V((BLOCK, BLOCK), BF),
        dma((9,)),
        V((64, 128), F32),
        V((NY, NZ, 64, 128), BF),
        V((NP * 64, 128), F32),
        V((128, 128), F32),
        V((64, SUFX), F32),
        V((KV * 128, 128), F32),
        V((KV * 128, 128), F32),
        V((KV * 128, 128), F32),
        V((128, 128), F32),
        V((KV, 2, 64, 128), BF),
        V((NP, 64, 128), BF),
        V((KV * 8, 128), F32),
        V((NP * 8, 128), F32),
        V((NP * PROJ_ROWS, 128), F32),
        V((NP, PROJ_ROWS, 128), BF),
        V((NP, PROJ_ROWS, 128), BF),
        V((2, PROJ_ROWS, 128), F32),
        V((PROJ_ROWS, 128), F32),
        V((NS, 16, 128), BF),
        V((NS, 16, 128), BF),
        V((NS * 16, 128), F32),
        V((6, 16, 128), F32),
        V((NY, NZ, 16, 768), BF),
        V((4, NZ, 2, 16, BLOCK), BF),
        V((4, 4, 2, 16, BLOCK), BF),
        V((4, 4, 2, 16, BLOCK), BF),
        V((4, 4, 2, 16, BLOCK), BF),
        V((4, NZ, 16, BLOCK), BF),
        V((4, NZ, 16, BLOCK), BF),
        V((4, NZ, 16, BLOCK), BF),
        V((NZ, 16, BLOCK), BF),
        V((NZ, 16, BLOCK), BF),
        dma((2, NZ)),
        dma((2, NY)),
        dma((2, NP)),
        dma((2, NP)),
        dma((2, NP)),
        dma((2, NS)),
        dma((2, NZ)),
        dma((2, NY)),
        dma((2, 4)),
        dma((2, 4, 4)),
        dma((2, 4, 4)),
        dma((2, 4)),
        dma((2, 4)),
        dma((2, NZ)),
    ]
    return pl.pallas_call(
        body,
        out_shape=(
            jax.ShapeDtypeStruct((2, D), BF),
            jax.ShapeDtypeStruct((16, BLOCK), BF),
        ),
        in_specs=[vmem] * 5 + [smem] * 2 + [hbm] * 6,
        out_specs=(vmem, vmem),
        scratch_shapes=scratch,
        compiler_params=pltpu.CompilerParams(
            collective_id=0, has_side_effects=True, vmem_limit_bytes=56 << 20
        ),
        name="layer",
    )(
        queries,
        fresh_key_value,
        residual,
        attn_gain.reshape(1, D),
        ffn_gain.reshape(1, D),
        suffix_len,
        sample_prompt,
        prompt_key_value,
        suffix_key_value,
        out_weight,
        gate_weight,
        up_weight,
        down_weight,
    )


def solution(mesh):
    return jax.shard_map(
        local,
        mesh=mesh,
        in_specs=(
            P(("prefix", "sample"), None),
            P(("prefix", "sample"), None),
            P(("prefix", "sample"), None, None),
            P("sample", None, "prefix", None),
            P(("prefix", "sample"), None, None, None),
            P(("prefix", "sample")),
            P(),
            P("prefix", None),
            P(),
            P(),
            P("sample", "prefix"),
            P("sample", "prefix"),
            P("prefix", "sample"),
        ),
        out_specs=(P(("prefix", "sample"), None), P("prefix", "sample")),
        check_vma=False,
    )
```

```python
import functools

import jax
import jax.numpy as jnp
from jax import lax
from jax.experimental import pallas as pl
from jax.experimental.pallas import tpu as pltpu
from jax.sharding import PartitionSpec as P

MESH = pl.DeviceIdType.MESH
SCALE = 168.0 ** (-0.5)
NEGATIVE = -1e30
EPSILON = 1e-06
BF = jnp.bfloat16
F32 = jnp.float32

NZ, NY, NX, NC = 8, 4, 4, 2
NP, NS = NZ * NY, NX * NC
HEADS, KV, WIDTH = 32, 16, 128
D = 5376
CHUNKS = D // 128
PROJ_ROWS = 88
BLOCK = 672
SUF = 192
SUFX = 208
Y_OFFSETS = X_OFFSETS = (1, 3, 2)
LAG = 2
NEAR = (0, 1, 7, 2, 6, 3, 5, 4)
FAR = (4, 5, 3, 6, 2, 7, 1, 0)
SCHEDULE = "a0 a1 b0 a2 b1 a3 b2 c0 b3 c1 d0 c2 d1 e0 c3 d2 e1 f0 d3 e2 f1 e3 f2 f3"


def dot(a, b):
    return jnp.dot(a, b, preferred_element_type=F32)


def dot_t(a, b):
    return lax.dot_general(a, b, (((1,), (1,)), ((), ())), preferred_element_type=F32)


def remote(src, dst, send_sem, recv_sem, device):
    return pltpu.make_async_remote_copy(
        src_ref=src,
        dst_ref=dst,
        send_sem=send_sem,
        recv_sem=recv_sem,
        device_id=device,
        device_id_type=MESH,
    )


def need(loads, n):
    loads[n].wait()


def body(*refs):
    ending, loads = [], []
    layer(ending, loads, *refs)
    for wait in ending:
        wait()


def layer(
    ending,
    loads,
    q_hbm,
    fresh_hbm,
    resid_hbm,
    again_hbm,
    fgain_hbm,
    slen_hbm,
    sprompt_hbm,
    pkv_hbm,
    skv_hbm,
    wout_hbm,
    wg_hbm,
    wu_hbm,
    wd_hbm,
    mid_hbm,
    out_hbm,
    q_ref,
    fresh_ref,
    resid_ref,
    again_ref,
    fgain_ref,
    slen_ref,
    sprompt_ref,
    mid_ref,
    out_ref,
    out_sem,
    pkv,
    skv,
    wout,
    wg,
    wu,
    wd,
    load_sem,
    q32,
    qall,
    qflat,
    sel,
    ssuf,
    msufx,
    lsufx,
    osufx,
    osend,
    orecv,
    stsend,
    strecv,
    ozsend,
    ozrecv,
    stzsend,
    stzrecv,
    pf,
    psend,
    precv,
    pzsend,
    pzrecv,
    gains,
    resid,
    e1send,
    e1recv,
    e1f,
    xf,
    xall,
    gu,
    gurecv,
    xs,
    xsrecv,
    hid,
    ysend,
    yrecv,
    zsend,
    zrecv,
    aq_z,
    aq_y,
    c_o,
    c_st,
    c_oz,
    c_stz,
    d_y,
    d_z,
    e_1,
    e_z,
    e_y,
    f_c,
    f_x,
    f_hx,
    f_hc,
    g_y,
    g_z,
):
    me = lax.axis_index("prefix")
    spos = lax.axis_index("sample")
    z, y = me // NY, me % NY
    x, c = spos // NC, spos % NC

    def send(src, dst, sem, recv, device):
        remote(src, dst, sem.at[0], sem.at[recv], device).start()

    def all_left(ref, sem):
        ending.append(remote(ref, ref, sem.at[0], sem.at[0], at_xc(x, c)).wait_send)

    def landed(ref, sem, recv):
        remote(ref, ref, sem.at[0], sem.at[recv], at_xc(x, c)).wait_recv()

    def at_zy(zz, yy):
        return {"prefix": zz * NY + yy, "sample": spos}

    def at_sample(s):
        return {"prefix": me, "sample": s}

    def at_xc(xx, cc):
        return {"prefix": me, "sample": xx * NC + cc}

    barrier = pltpu.get_barrier_semaphore()

    for i in range(1, NZ):
        pl.semaphore_signal(
            barrier, 1, device_id=at_zy(lax.rem(z + i, NZ), y), device_id_type=MESH
        )
    for i in range(1, NY):
        pl.semaphore_signal(
            barrier, 1, device_id=at_zy(z, lax.rem(y + i, NY)), device_id_type=MESH
        )

    @pl.loop(1, NS)
    def _(i):
        pl.semaphore_signal(
            barrier, 1, device_id=at_sample(lax.rem(spos + i, NS)), device_id_type=MESH
        )

    def load(src, dst):
        cp = pltpu.make_async_copy(src, dst, load_sem.at[len(loads)])
        cp.start()
        loads.append(cp)

    load(q_hbm, q_ref)
    load(sprompt_hbm, sprompt_ref)
    load(slen_hbm, slen_ref)
    load(fresh_hbm, fresh_ref)
    load(resid_hbm, resid_ref)
    load(again_hbm, again_ref)
    load(fgain_hbm, fgain_ref)
    for t in range(2):
        for s in range(2):
            load(skv_hbm.at[s, t], skv.at[s, t, pl.ds(0, SUF)])
    load(pkv_hbm, pkv)

    need(loads, 0)
    for h in range(HEADS):
        q32[2 * h : 2 * h + 2, :] = q_ref[:, h * 128 : (h + 1) * 128].astype(F32)
    qall[0, 0] = q32[...].astype(BF)

    pl.semaphore_wait(barrier, NZ - 1 + NY - 1 + NS - 1)

    def spread(buf, sem_z, sem_y):
        def to_y(n):
            for i in Y_OFFSETS:
                there = at_zy(z, lax.rem(y + i, NY))
                send(buf.at[n, 0], buf.at[n, (-i) % NY], sem_y, 1 + n, there)

        def start():
            for n in range(NZ - 1, 0, -1):
                slot = NEAR.index((-NEAR[n]) % NZ)
                there = at_zy(lax.rem(z + NEAR[n], NZ), y)
                send(buf.at[0, 0], buf.at[slot, 0], sem_z, 1 + slot, there)
            to_y(0)
            all_left(buf.at[pl.ds(1, NZ - 1), 0], sem_z)
            all_left(buf.at[pl.ds(0, NZ), pl.ds(1, NY - 1)], sem_y)

        def pass_on(n):
            landed(buf.at[n, 0], sem_z, 1 + n)
            to_y(n)

        def take(n):
            landed(buf.at[n, pl.ds(1, NY - 1)], sem_y, 1 + n)

        return start, pass_on, take

    q_start, q_pass, q_take = spread(qall, aq_z, aq_y)
    q_start()

    need(loads, 1)
    @pl.loop(0, 2 * NP)
    def _(r):
        value = sprompt_ref[lax.rem(r, NP) * 16 + 2 * spos + r // NP] - 2 * spos
        row = jnp.full((1, 128), value, jnp.int32).astype(F32)
        sel[pl.ds(r, 1), :] = row
        sel[pl.ds(r + 2 * NP, 1), :] = row

    msufx[...] = jnp.full(msufx.shape, NEGATIVE, F32)
    q_pass(1)

    need(loads, 3)
    first_row = lax.broadcasted_iota(jnp.int32, (16, 2048), 0) == 0
    for s in range(2):
        for t in range(2):
            row = jnp.broadcast_to(fresh_ref[s, t : t + 1, :].astype(F32), (16, 2048))
            skv[s, t, SUF:SUFX, :] = jnp.where(first_row, row, 0.0).astype(BF)
    q_pass(2)
    for s in range(2):
        need(loads, 7 + s)

    def suffix_scores(k):
        lanes = slice(k * 128, (k + 1) * 128)
        rows = q32[4 * k : 4 * k + 4, :].astype(BF)
        odd = lax.broadcasted_iota(jnp.int32, (4, SUFX), 0) % 2 == 1
        ssuf[4 * k : 4 * k + 4, :] = jnp.where(
            odd, dot_t(rows, skv[1, 0, :, lanes]), dot_t(rows, skv[0, 0, :, lanes])
        )

    for k in range(KV // 2):
        suffix_scores(k)
    q_pass(3)
    for k in range(KV // 2, KV):
        suffix_scores(k)
    q_pass(4)
    odd = lax.broadcasted_iota(jnp.int32, (64, SUFX), 0) % 2 == 1
    slot = lax.broadcasted_iota(jnp.int32, (64, SUFX), 1)
    need(loads, 2)
    length = jnp.where(odd, slen_ref[1], slen_ref[0])
    scores = jnp.where((slot < length) | (slot == SUF), ssuf[...] * SCALE, NEGATIVE)
    msuf = jnp.max(scores, axis=1, keepdims=True)
    expo = jnp.exp(scores - msuf)
    lsuf = jnp.broadcast_to(jnp.sum(expo, axis=1, keepdims=True), (64, 128))
    msuf = jnp.broadcast_to(msuf, (64, 128))
    even_w = jnp.where(odd, 0.0, expo)
    odd_w = jnp.where(odd, expo, 0.0)
    q_pass(5)
    q_pass(6)
    q_pass(7)
    lsufx[...] = jnp.zeros(lsufx.shape, F32)
    osufx[...] = jnp.zeros(osufx.shape, F32)
    for s in range(2):
        need(loads, 9 + s)
    for k in range(KV):
        lanes = slice(k * 128, (k + 1) * 128)
        part = slice(4 * k, 4 * k + 4)
        o = dot(even_w[part].astype(BF), skv[0, 1, :, lanes]) + dot(
            odd_w[part].astype(BF), skv[1, 1, :, lanes]
        )
        for g in range(2):
            for s in range(2):
                src = 4 * k + 2 * g + s
                dst = k * 128 + g * 64 + s * 32 + me
                msufx[pl.ds(dst, 1), :] = msuf[src : src + 1]
                lsufx[pl.ds(dst, 1), :] = lsuf[src : src + 1]
                osufx[pl.ds(dst, 1), :] = o[2 * g + s : 2 * g + s + 1]

    for n in range(NZ):
        q_take(n)
        for i in range(NY):
            owner = lax.rem(z + NEAR[n], NZ) * NY + lax.rem(y + i, NY)
            qflat[pl.ds(pl.multiple_of(owner * 64, 64), 64), :] = qall[n, i].astype(F32)

    load(wout_hbm, wout)
    load(wg_hbm, wg)
    load(wu_hbm, wu)
    load(wd_hbm, wd)

    need(loads, 11)
    chosen = sel[...] > 0.5
    lane = lax.broadcasted_iota(jnp.int32, (128, 128), 1)
    diagonal = lax.broadcasted_iota(jnp.int32, (64, 64), 0) == lax.broadcasted_iota(
        jnp.int32, (64, 64), 1
    )

    def attend(k):
        lanes = pl.ds(pl.multiple_of(k * 128, 128), 128)
        rows = pl.ds(pl.multiple_of(k * 128, 128), 128)
        q = jnp.concatenate(
            [qflat[pl.ds(4 * k + t, 32, stride=64), :] for t in range(4)], axis=0
        ).astype(BF)
        scores = jnp.where(chosen, dot_t(q, pkv[1, 0, :, lanes]), dot_t(q, pkv[0, 0, :, lanes]))
        scores = scores * SCALE
        ms = msufx[rows, :]
        m = jnp.maximum(ms, jnp.max(scores, axis=1, keepdims=True))
        expo = jnp.exp(scores - m)
        a = jnp.exp(ms - m)
        total = jnp.sum(expo, axis=1, keepdims=True) + a * lsufx[rows, :]
        w0 = jnp.where(chosen, 0.0, expo).astype(BF)
        w1 = jnp.where(chosen, expo, 0.0).astype(BF)
        o = dot(w0, pkv[0, 1, :, lanes]) + dot(w1, pkv[1, 1, :, lanes]) + a * osufx[rows, :]
        return o.astype(BF), m, total

    def o_to_y(n, i):
        yy = lax.rem(y + i, NY)
        send(osend.at[n, yy], orecv.at[n, (-i) % NY], c_o, 1 + n, at_zy(z, yy))
        send(stsend.at[n], strecv.at[n, (-i) % NY], c_st, 1 + n, at_zy(z, yy))

    def blend(weights, parts):
        total = None
        for low in (False, True):
            pieces = []
            for w in weights:
                w = w[:, :64]
                high = w.astype(BF).astype(F32)
                w = w - high if low else high
                pieces.append(jnp.where(diagonal, jnp.broadcast_to(w, (64, 64)), 0.0).astype(BF))
            term = dot(jnp.concatenate(pieces, axis=1), jnp.concatenate(parts, axis=0))
            total = term if total is None else total + term
        return total

    odd_y = jnp.zeros((1, 128), jnp.int32) + lax.rem(y, 2) == 1
    stat_row = 2 * (y // 2)

    def merge(n):
        maxima, totals, parts = [], [], []
        landed(orecv.at[n, pl.ds(1, NY - 1)], c_o, 1 + n)
        landed(strecv.at[n, pl.ds(1, NY - 1)], c_st, 1 + n)
        for i in range(NY):
            if i:
                parts.append(orecv[n, i])
                m = strecv[n, i, pl.ds(stat_row, 1), :]
                total = strecv[n, i, pl.ds(stat_row + 1, 1), :]
            else:
                parts.append(osend[n, y])
                m = stsend[n, pl.ds(stat_row, 1), :]
                total = stsend[n, pl.ds(stat_row + 1, 1), :]
            maxima.append(jnp.where(odd_y, pltpu.roll(m, 64, 1), m))
            totals.append(jnp.where(odd_y, pltpu.roll(total, 64, 1), total))
        top = functools.reduce(jnp.maximum, maxima)
        weights = [jnp.exp(m - top) for m in maxima]
        total = sum(w * t for w, t in zip(weights, totals))
        ozsend[n] = blend(weights, parts).astype(BF)
        first = lax.broadcasted_iota(jnp.int32, (8, 128), 0) == 0
        stzsend[n] = jnp.where(
            first, jnp.broadcast_to(top, (8, 128)), jnp.broadcast_to(total, (8, 128))
        )
        if FAR[n]:
            there = at_zy(lax.rem(z + FAR[n], NZ), y)
            send(ozsend.at[n], ozrecv.at[n], c_oz, 1 + n, there)
            send(stzsend.at[n], stzrecv.at[n], c_stz, 1 + n, there)

    for n in range(NZ):
        zz = lax.rem(z + FAR[n], NZ)
        o0, m0, t0 = attend(2 * zz)
        o1, m1, t1 = attend(2 * zz + 1)
        for g in range(2):
            osend[n, g] = o0[g * 64 : (g + 1) * 64]
            osend[n, 2 + g] = o1[g * 64 : (g + 1) * 64]
        stats = jnp.where(
            lane == 0, m0, jnp.where(lane == 1, t0, jnp.where(lane == 2, m1, t1))
        )
        stsend[n] = stats.T[0:8]
        for i in Y_OFFSETS:
            o_to_y(n, i)
        if n >= LAG:
            merge(n - LAG)
    for n in range(NZ - LAG, NZ):
        merge(n)

    all_left(orecv.at[pl.ds(0, NZ), pl.ds(1, NY - 1)], c_o)
    all_left(strecv.at[pl.ds(0, NZ), pl.ds(1, NY - 1)], c_st)
    all_left(ozrecv.at[pl.ds(0, NZ - 1)], c_oz)
    all_left(stzrecv.at[pl.ds(0, NZ - 1)], c_stz)

    maxima, totals, parts = [], [], []
    for n in range(NZ - 1):
        landed(ozrecv.at[n], c_oz, 1 + n)
        landed(stzrecv.at[n], c_stz, 1 + n)
        maxima.append(stzrecv[n, 0:1, :])
        totals.append(stzrecv[n, 1:2, :])
        parts.append(ozrecv[n])
    maxima.append(stzsend[NZ - 1, 0:1, :])
    totals.append(stzsend[NZ - 1, 1:2, :])
    parts.append(ozsend[NZ - 1])
    top = functools.reduce(jnp.maximum, maxima)
    weights = [jnp.exp(m - top) for m in maxima]
    total = sum(w * t for w, t in zip(weights, totals))
    attended = blend([w / total for w in weights], parts).astype(BF)

    need(loads, 12)
    for j in range(CHUNKS // 2):
        r = dot(attended, wout[:, 256 * j : 256 * (j + 1)])
        for t in range(2):
            for s in range(2):
                pf[pl.ds(4 * j + 2 * t + s, NP, stride=PROJ_ROWS), :] = r[
                    s * 32 : (s + 1) * 32, t * 128 : (t + 1) * 128
                ]
    for s in range(2 * CHUNKS, PROJ_ROWS):
        pf[pl.ds(s, NP, stride=PROJ_ROWS), :] = jnp.zeros((NP, 128), F32)

    def reduced(n_z, y_out, y_in, z_out, z_in, sem_y, sem_z):
        def to_y(n, i):
            there = at_zy(z, lax.rem(y + i, NY))
            send(y_out.at[n, i], y_in.at[n, (-i) % NY], sem_y, 1 + n, there)

        def add_y(n):
            landed(y_in.at[n, pl.ds(1, NY - 1)], sem_y, 1 + n)
            total = y_out[n, 0].astype(F32)
            for i in Y_OFFSETS:
                total = total + y_in[n, i].astype(F32)
            return total

        def to_z(n, total):
            z_out[n] = total.astype(BF)
            there = at_zy(lax.rem(z + n_z[n], NZ), y)
            send(z_out.at[n], z_in.at[n], sem_z, 1 + n, there)

        def add_z(n):
            landed(z_in.at[n], sem_z, 1 + n)
            return z_in[n].astype(F32)

        all_left(y_in.at[pl.ds(0, NZ), pl.ds(1, NY - 1)], sem_y)
        all_left(z_in.at[pl.ds(0, NZ - 1)], sem_z)
        return to_y, add_y, to_z, add_z

    p_to_y, p_add_y, p_to_z, p_add_z = reduced(FAR, psend, precv, pzsend, pzrecv, d_y, d_z)
    for n in range(NZ):
        for i in Y_OFFSETS + (0,):
            o = lax.rem(z + FAR[n], NZ) * NY + lax.rem(y + i, NY)
            start = pl.multiple_of(o * PROJ_ROWS, 8)
            psend[n, i] = pf[pl.ds(start, PROJ_ROWS), :].astype(BF)
            if i:
                p_to_y(n, i)
    for n in (4, 5, 6):
        need(loads, n)
    for j in range(CHUNKS):
        cols = slice(j * 128, (j + 1) * 128)
        resid[2 * j : 2 * j + 2, :] = resid_ref[:, cols].astype(F32)
        gains[0, 2 * j : 2 * j + 2, :] = jnp.broadcast_to(again_ref[cols].reshape(1, 128), (2, 128))
        gains[1, 2 * j : 2 * j + 2, :] = jnp.broadcast_to(fgain_ref[cols].reshape(1, 128), (2, 128))
    for n in range(NZ - 1):
        p_to_z(n, p_add_y(n))
    projected = p_add_y(NZ - 1)
    for n in range(NZ - 1):
        projected = projected + p_add_z(n)

    row = lax.broadcasted_iota(jnp.int32, (PROJ_ROWS, 128), 0)
    odd = row % 2 == 1
    real = row < 2 * CHUNKS

    def normed(values, gain):
        square = jnp.where(real, values * values, 0.0)
        second = jnp.sum(jnp.where(odd, square, 0.0))
        first = jnp.sum(jnp.where(odd, 0.0, square))
        inv = jnp.where(odd, second, first) * (1.0 / D) + EPSILON
        return values * lax.rsqrt(inv) * gain

    midway = (resid[...] + normed(projected, gains[0])).astype(BF)
    settled = midway.astype(F32)
    ffn_in = normed(settled, gains[1]).astype(BF).astype(F32)
    ffn_in = jnp.where(real, ffn_in, 0.0)

    lane = lax.broadcasted_iota(jnp.int32, (12, 128), 1)
    rolled = [ffn_in if o == 0 else pltpu.roll(ffn_in, 128 - o, 1) for o in (0, 32, 64, 96)]
    for b in range(NS):
        o, j0 = 32 * (b % 4), (21 * b) // 4
        v = rolled[b % 4]
        piece = v[2 * j0 : 2 * j0 + 12]
        if o:
            piece = jnp.where(lane < 128 - o, piece, v[2 * j0 + 2 : 2 * j0 + 14])
        e1send[b] = jnp.concatenate([piece, jnp.zeros((4, 128), F32)], axis=0).astype(BF)

    for i in range(1, NS):
        b = lax.rem(spos + i, NS)
        send(e1send.at[b], e1recv.at[spos], e_1, 1, at_sample(b))
    all_left(e1send.at[pl.ds(1, NS - 1)], e_1)
    e1recv[spos] = e1send[spos]
    for j in range(CHUNKS):
        mid_ref[:, j * 128 : (j + 1) * 128] = settled[2 * j : 2 * j + 2].astype(BF)
    mid_copy = pltpu.make_async_copy(mid_ref, mid_hbm, out_sem.at[0])
    mid_copy.start()
    ending.append(mid_copy.wait)
    landed(e1recv.at[pl.ds(1, NS - 1)], e_1, 1)
    for b in range(NS):
        e1f[16 * b : 16 * (b + 1), :] = e1recv[b].astype(F32)
    for i in range(6):
        for s in range(2):
            xf[i, pl.ds(s, 8, stride=2), :] = e1f[pl.ds(2 * i + s, 8, stride=16), :]
    for i in range(6):
        xall[0, 0, :, i * 128 : (i + 1) * 128] = xf[i].astype(BF)

    x_start, x_pass, x_take = spread(xall, e_z, e_y)
    x_start()
    for n in (13, 14, 15):
        need(loads, n)

    def stage_a(ci):
        for n in (2 * ci, 2 * ci + 1):
            x_take(n)
        v = xall[2 * ci : 2 * ci + 2].reshape(128, 768)[:, :BLOCK]
        gu[ci, :, 0] = dot(v, wg[...]).astype(BF).reshape(NZ, 16, BLOCK)
        gu[ci, :, 1] = dot(v, wu[...]).astype(BF).reshape(NZ, 16, BLOCK)
        send(gu.at[ci, pl.ds(4 * (1 - c), 4)], gurecv.at[ci], f_c, 1 + ci, at_xc(x, 1 - c))

    def stage_b(ci):
        landed(gurecv.at[ci], f_c, 1 + ci)
        for xx in range(NX):
            xs[ci, xx] = (gu[ci, 4 * c + xx].astype(F32) + gurecv[ci, xx].astype(F32)).astype(BF)
        for i in X_OFFSETS:
            xx = lax.rem(x + i, NX)
            send(xs.at[ci, xx], xsrecv.at[ci, i], f_x, 1 + ci, at_xc(xx, c))

    def stage_c(ci):
        landed(xsrecv.at[ci, pl.ds(1, NX - 1)], f_x, 1 + ci)
        total = xs[ci, x].astype(F32)
        for i in X_OFFSETS:
            total = total + xsrecv[ci, i].astype(F32)
        own = hid.at[ci, 4 * c + x]
        own[...] = (jax.nn.gelu(total[0], approximate=True) * total[1]).astype(BF)
        for i in X_OFFSETS:
            send(own, own, f_hx, 1 + ci, at_xc(lax.rem(x + i, NX), c))

    def stage_d(ci):
        landed(hid.at[ci, pl.ds(0, NX - 1)], f_hx, 1 + ci)
        half = hid.at[ci, pl.ds(4 * c, 4)]
        send(half, half, f_hc, 1 + ci, at_xc(x, 1 - c))

    all_left(gurecv, f_c)
    all_left(xsrecv.at[pl.ds(0, 4), pl.ds(1, NX - 1)], f_x)
    all_left(hid.at[pl.ds(0, 4), pl.ds(0, NX - 1)], f_hx)
    all_left(hid.at[pl.ds(0, 4), pl.ds(0, 4)], f_hc)
    y_to_y, y_add_y, y_to_z, y_add_z = reduced(NEAR, ysend, yrecv, zsend, zrecv, g_y, g_z)

    def stage_e(ci):
        landed(hid.at[ci, pl.ds(4 * (1 - c), 4)], f_hc, 1 + ci)
        two = dot(hid[ci].reshape(128, BLOCK), wd[...]).astype(BF).reshape(2, NY, 16, BLOCK)
        ysend[2 * ci : 2 * ci + 2] = two
        for n in (2 * ci, 2 * ci + 1):
            for i in Y_OFFSETS:
                y_to_y(n, i)

    def stage_f(ci):
        for n in (2 * ci, 2 * ci + 1):
            if n:
                y_to_z(n, y_add_y(n))

    for n in range(1, NZ):
        x_pass(n)
    stages = {"a": stage_a, "b": stage_b, "c": stage_c, "d": stage_d, "e": stage_e, "f": stage_f}
    for name in SCHEDULE.split():
        stages[name[0]](int(name[1]))
    total = y_add_y(0)
    for n in range(1, NZ):
        total = total + y_add_z(n)
    out_ref[...] = total.astype(BF)
    out_copy = pltpu.make_async_copy(out_ref, out_hbm, out_sem.at[1])
    out_copy.start()
    ending.append(out_copy.wait)


def local(
    residual,
    queries,
    fresh_key_value,
    prompt_key_value,
    suffix_key_value,
    suffix_len,
    sample_prompt,
    out_weight,
    attn_gain,
    ffn_gain,
    gate_weight,
    up_weight,
    down_weight,
):
    hbm = pl.BlockSpec(memory_space=pl.ANY)
    V = pltpu.VMEM
    dma = pltpu.SemaphoreType.DMA
    scratch = [
        V((2, HEADS * WIDTH), BF),
        V((2, 2, KV * WIDTH), BF),
        V((2, D), BF),
        V((D,), F32),
        V((D,), F32),
        pltpu.SMEM((2,), jnp.int32),
        pltpu.SMEM((2 * NP * NS,), jnp.int32),
        V((2, D), BF),
        V((16, BLOCK), BF),
        dma((2,)),
        V((2, 2, 128, 2048), BF),
        V((2, 2, SUFX, 2048), BF),
        V((128, D), BF),
        V((BLOCK, BLOCK), BF),
        V((BLOCK, BLOCK), BF),
        V((BLOCK, BLOCK), BF),
        dma((16,)),
        V((64, 128), F32),
        V((NZ, NY, 64, 128), BF),
        V((NP * 64, 128), F32),
        V((128, 128), F32),
        V((64, SUFX), F32),
        V((KV * 128, 128), F32),
        V((KV * 128, 128), F32),
        V((KV * 128, 128), F32),
        V((NZ, NY, 64, 128), BF),
        V((NZ, NY, 64, 128), BF),
        V((NZ, 8, 128), F32),
        V((NZ, NY, 8, 128), F32),
        V((NZ, 64, 128), BF),
        V((NZ, 64, 128), BF),
        V((NZ, 8, 128), F32),
        V((NZ, 8, 128), F32),
        V((NP * PROJ_ROWS, 128), F32),
        V((NZ, NY, PROJ_ROWS, 128), BF),
        V((NZ, NY, PROJ_ROWS, 128), BF),
        V((NZ, PROJ_ROWS, 128), BF),
        V((NZ, PROJ_ROWS, 128), BF),
        V((2, PROJ_ROWS, 128), F32),
        V((PROJ_ROWS, 128), F32),
        V((NS, 16, 128), BF),
        V((NS, 16, 128), BF),
        V((NS * 16, 128), F32),
        V((6, 16, 128), F32),
        V((NZ, NY, 16, 768), BF),
        V((4, NZ, 2, 16, BLOCK), BF),
        V((4, 4, 2, 16, BLOCK), BF),
        V((4, 4, 2, 16, BLOCK), BF),
        V((4, 4, 2, 16, BLOCK), BF),
        V((4, NZ, 16, BLOCK), BF),
        V((NZ, NY, 16, BLOCK), BF),
        V((NZ, NY, 16, BLOCK), BF),
        V((NZ, 16, BLOCK), BF),
        V((NZ, 16, BLOCK), BF),
        dma((1 + NZ,)),
        dma((1 + NZ,)),
        dma((1 + NZ,)),
        dma((1 + NZ,)),
        dma((1 + NZ,)),
        dma((1 + NZ,)),
        dma((1 + NZ,)),
        dma((1 + NZ,)),
        dma((2,)),
        dma((1 + NZ,)),
        dma((1 + NZ,)),
        dma((5,)),
        dma((5,)),
        dma((5,)),
        dma((5,)),
        dma((1 + NZ,)),
        dma((1 + NZ,)),
    ]
    return pl.pallas_call(
        body,
        out_shape=(
            jax.ShapeDtypeStruct((2, D), BF),
            jax.ShapeDtypeStruct((16, BLOCK), BF),
        ),
        in_specs=[hbm] * 13,
        out_specs=(hbm, hbm),
        scratch_shapes=scratch,
        compiler_params=pltpu.CompilerParams(
            collective_id=0, has_side_effects=True, vmem_limit_bytes=56 << 20
        ),
        name="layer",
    )(
        queries,
        fresh_key_value,
        residual,
        attn_gain,
        ffn_gain,
        suffix_len,
        sample_prompt,
        prompt_key_value,
        suffix_key_value,
        out_weight,
        gate_weight,
        up_weight,
        down_weight,
    )


def solution(mesh):
    return jax.shard_map(
        local,
        mesh=mesh,
        in_specs=(
            P(("prefix", "sample"), None),
            P(("prefix", "sample"), None),
            P(("prefix", "sample"), None, None),
            P("sample", None, "prefix", None),
            P(("prefix", "sample"), None, None, None),
            P(("prefix", "sample")),
            P(),
            P("prefix", None),
            P(),
            P(),
            P("sample", "prefix"),
            P("sample", "prefix"),
            P("prefix", "sample"),
        ),
        out_specs=(P(("prefix", "sample"), None), P("prefix", "sample")),
        check_vma=False,
    )
```

```python
import functools

import jax
import jax.numpy as jnp
from jax import lax
from jax.experimental import pallas as pl
from jax.experimental.pallas import tpu as pltpu
from jax.sharding import PartitionSpec as P

MESH = pl.DeviceIdType.MESH
SCALE = 168.0 ** (-0.5)
NEGATIVE = -1e30
EPSILON = 1e-06
BF = jnp.bfloat16
F32 = jnp.float32

NZ, NY, NX, NC = 8, 4, 4, 2
NP, NS = NZ * NY, NX * NC
HEADS, KV, WIDTH = 32, 16, 128
D = 5376
CHUNKS = D // 128
PROJ_ROWS = 88
BLOCK = 672
SUF = 192
SUFX = 208
Y_OFFSETS = X_OFFSETS = (1, 3, 2)
LAG = 6
NEAR = (0, 1, 7, 2, 6, 3, 5, 4)
FFN_ORDER = (0, 4, 2, 3, 6, 5, 1, 7)
FAR = (4, 5, 3, 6, 2, 7, 1, 0)
TURNS = 4
SCHEDULE = (
    ("a", 0), ("a", 1), ("a", 2), ("a", 3),
    ("c", 0), ("c", 1), ("c", 2), ("c", 3),
    ("e", 0), ("e", 1), ("e", 2), ("e", 3),
    ("f", 0), ("f", 1), ("f", 2), ("f", 3),
)


def dot(a, b):
    return jnp.dot(a, b, preferred_element_type=F32)


def dot_t(a, b):
    return lax.dot_general(a, b, (((1,), (1,)), ((), ())), preferred_element_type=F32)


def remote(src, dst, send_sem, recv_sem, device):
    return pltpu.make_async_remote_copy(
        src_ref=src,
        dst_ref=dst,
        send_sem=send_sem,
        recv_sem=recv_sem,
        device_id=device,
        device_id_type=MESH,
    )


def need(loads, n):
    loads[n].wait()


def body(*refs):
    ending, loads = [], []
    layer(ending, loads, *refs)
    for wait in ending:
        wait()


def layer(
    ending,
    loads,
    q_hbm,
    fresh_hbm,
    resid_hbm,
    again_hbm,
    fgain_hbm,
    slen_hbm,
    sprompt_hbm,
    pkv_hbm,
    skv_hbm,
    wout_hbm,
    wg_hbm,
    wu_hbm,
    wd_hbm,
    mid_hbm,
    out_hbm,
    q_ref,
    fresh_ref,
    resid_ref,
    again_ref,
    fgain_ref,
    slen_ref,
    sprompt_ref,
    mid_ref,
    out_ref,
    out_sem,
    pkv,
    skv,
    wout,
    ffw,
    load_sem,
    q32,
    qall,
    qflat,
    sel,
    ssuf,
    msufx,
    lsufx,
    osufx,
    osend,
    orecv,
    stsend,
    strecv,
    ozsend,
    ozrecv,
    stzsend,
    stzrecv,
    pf,
    psend,
    precv,
    pzsend,
    pzrecv,
    gains,
    resid,
    e1send,
    e1recv,
    e1f,
    xf,
    xown,
    xall,
    gu,
    gurecv,
    hid,
    ysend,
    yrecv,
    zsend,
    zrecv,
    w_c,
    aq_z,
    aq_y,
    c_o,
    c_st,
    c_oz,
    c_stz,
    d_y,
    d_z,
    e_1,
    e_z,
    e_y,
    f_x,
    f_hx,
    g_y,
    g_z,
):
    me = lax.axis_index("prefix")
    spos = lax.axis_index("sample")
    z, y = me // NY, me % NY
    x, c = spos // NC, spos % NC

    def send(src, dst, sem, recv, device):
        remote(src, dst, sem.at[0], sem.at[recv], device).start()

    def all_left(ref, sem):
        ending.append(remote(ref, ref, sem.at[0], sem.at[0], at_xc(x, c)).wait_send)

    def landed(ref, sem, recv):
        remote(ref, ref, sem.at[0], sem.at[recv], at_xc(x, c)).wait_recv()

    def at_zy(zz, yy):
        return {"prefix": zz * NY + yy, "sample": spos}

    def at_zyc(zz, yy, cc):
        return {"prefix": zz * NY + yy, "sample": x * NC + cc}

    def at_sample(s):
        return {"prefix": me, "sample": s}

    def at_xc(xx, cc):
        return {"prefix": me, "sample": xx * NC + cc}

    barrier = pltpu.get_barrier_semaphore()

    for i in range(1, NZ):
        for cc in range(NC):
            there = at_zyc(lax.rem(z + i, NZ), y, cc)
            pl.semaphore_signal(barrier, 1, device_id=there, device_id_type=MESH)
    for i in range(1, NY):
        pl.semaphore_signal(
            barrier, 1, device_id=at_zy(z, lax.rem(y + i, NY)), device_id_type=MESH
        )

    @pl.loop(1, NS)
    def _(i):
        pl.semaphore_signal(
            barrier, 1, device_id=at_sample(lax.rem(spos + i, NS)), device_id_type=MESH
        )

    def load(src, dst):
        cp = pltpu.make_async_copy(src, dst, load_sem.at[len(loads)])
        cp.start()
        loads.append(cp)

    load(q_hbm, q_ref)
    load(sprompt_hbm, sprompt_ref)
    load(slen_hbm, slen_ref)
    load(fresh_hbm, fresh_ref)
    load(resid_hbm, resid_ref)
    load(again_hbm, again_ref)
    load(fgain_hbm, fgain_ref)
    for t in range(2):
        for s in range(2):
            load(skv_hbm.at[s, t], skv.at[s, t, pl.ds(0, SUF)])
    load(pkv_hbm, pkv)

    need(loads, 0)
    for h in range(HEADS):
        q32[2 * h : 2 * h + 2, :] = q_ref[:, h * 128 : (h + 1) * 128].astype(F32)
    qall[0, 0] = q32[...].astype(BF)

    pl.semaphore_wait(barrier, NC * (NZ - 1) + NY - 1 + NS - 1)

    def spread(order, buf, sem_z, sem_y):
        def to_y(n):
            for i in Y_OFFSETS:
                there = at_zy(z, lax.rem(y + i, NY))
                send(buf.at[n, 0], buf.at[n, (-i) % NY], sem_y, 1 + n, there)

        def start():
            for n in range(NZ - 1, 0, -1):
                slot = order.index((-order[n]) % NZ)
                there = at_zy(lax.rem(z + order[n], NZ), y)
                send(buf.at[0, 0], buf.at[slot, 0], sem_z, 1 + slot, there)
            to_y(0)
            all_left(buf.at[pl.ds(1, NZ - 1), 0], sem_z)
            all_left(buf.at[pl.ds(0, NZ), pl.ds(1, NY - 1)], sem_y)

        def pass_on(n):
            landed(buf.at[n, 0], sem_z, 1 + n)
            to_y(n)

        def take(n):
            landed(buf.at[n, pl.ds(1, NY - 1)], sem_y, 1 + n)

        return start, pass_on, take

    q_start, q_pass, q_take = spread(NEAR, qall, aq_z, aq_y)
    q_start()

    need(loads, 1)
    @pl.loop(0, 2 * NP)
    def _(r):
        value = sprompt_ref[lax.rem(r, NP) * 16 + 2 * spos + r // NP] - 2 * spos
        row = jnp.full((1, 128), value, jnp.int32).astype(F32)
        sel[pl.ds(r, 1), :] = row
        sel[pl.ds(r + 2 * NP, 1), :] = row

    msufx[...] = jnp.full(msufx.shape, NEGATIVE, F32)
    q_pass(1)

    need(loads, 3)
    first_row = lax.broadcasted_iota(jnp.int32, (16, 2048), 0) == 0
    for s in range(2):
        for t in range(2):
            row = jnp.broadcast_to(fresh_ref[s, t : t + 1, :].astype(F32), (16, 2048))
            skv[s, t, SUF:SUFX, :] = jnp.where(first_row, row, 0.0).astype(BF)
    q_pass(2)
    for s in range(2):
        need(loads, 7 + s)

    def suffix_scores(k):
        lanes = slice(k * 128, (k + 1) * 128)
        rows = q32[4 * k : 4 * k + 4, :].astype(BF)
        odd = lax.broadcasted_iota(jnp.int32, (4, SUFX), 0) % 2 == 1
        ssuf[4 * k : 4 * k + 4, :] = jnp.where(
            odd, dot_t(rows, skv[1, 0, :, lanes]), dot_t(rows, skv[0, 0, :, lanes])
        )

    for k in range(KV // 2):
        suffix_scores(k)
    q_pass(3)
    for k in range(KV // 2, KV):
        suffix_scores(k)
    q_pass(4)
    odd = lax.broadcasted_iota(jnp.int32, (64, SUFX), 0) % 2 == 1
    slot = lax.broadcasted_iota(jnp.int32, (64, SUFX), 1)
    need(loads, 2)
    length = jnp.where(odd, slen_ref[1], slen_ref[0])
    scores = jnp.where((slot < length) | (slot == SUF), ssuf[...] * SCALE, NEGATIVE)
    msuf = jnp.max(scores, axis=1, keepdims=True)
    expo = jnp.exp(scores - msuf)
    lsuf = jnp.broadcast_to(jnp.sum(expo, axis=1, keepdims=True), (64, 128))
    msuf = jnp.broadcast_to(msuf, (64, 128))
    even_w = jnp.where(odd, 0.0, expo)
    odd_w = jnp.where(odd, expo, 0.0)
    q_pass(5)
    q_pass(6)
    q_pass(7)
    lsufx[...] = jnp.zeros(lsufx.shape, F32)
    osufx[...] = jnp.zeros(osufx.shape, F32)
    for s in range(2):
        need(loads, 9 + s)
    for k in range(KV):
        lanes = slice(k * 128, (k + 1) * 128)
        part = slice(4 * k, 4 * k + 4)
        o = dot(even_w[part].astype(BF), skv[0, 1, :, lanes]) + dot(
            odd_w[part].astype(BF), skv[1, 1, :, lanes]
        )
        for g in range(2):
            for s in range(2):
                src = 4 * k + 2 * g + s
                dst = k * 128 + g * 64 + s * 32 + me
                msufx[pl.ds(dst, 1), :] = msuf[src : src + 1]
                lsufx[pl.ds(dst, 1), :] = lsuf[src : src + 1]
                osufx[pl.ds(dst, 1), :] = o[2 * g + s : 2 * g + s + 1]

    for n in range(NZ):
        q_take(n)
        for i in range(NY):
            owner = lax.rem(z + NEAR[n], NZ) * NY + lax.rem(y + i, NY)
            qflat[pl.ds(pl.multiple_of(owner * 64, 64), 64), :] = qall[n, i].astype(F32)

    load(wout_hbm, wout)
    for t, ref in enumerate((wg_hbm, wu_hbm, wd_hbm)):
        load(ref, ffw.at[t, c])
        send(ref, ffw.at[t, c], w_c, 1 + t, at_xc(x, 1 - c))
    all_left(ffw.at[pl.ds(0, 3), 0], w_c)

    need(loads, 11)
    chosen = sel[...] > 0.5
    lane = lax.broadcasted_iota(jnp.int32, (128, 128), 1)
    diagonal = lax.broadcasted_iota(jnp.int32, (64, 64), 0) == lax.broadcasted_iota(
        jnp.int32, (64, 64), 1
    )

    def attend(k):
        lanes = pl.ds(pl.multiple_of(k * 128, 128), 128)
        rows = pl.ds(pl.multiple_of(k * 128, 128), 128)
        q = jnp.concatenate(
            [qflat[pl.ds(4 * k + t, 32, stride=64), :] for t in range(4)], axis=0
        ).astype(BF)
        scores = jnp.where(chosen, dot_t(q, pkv[1, 0, :, lanes]), dot_t(q, pkv[0, 0, :, lanes]))
        scores = scores * SCALE
        ms = msufx[rows, :]
        m = jnp.maximum(ms, jnp.max(scores, axis=1, keepdims=True))
        expo = jnp.exp(scores - m)
        a = jnp.exp(ms - m)
        total = jnp.sum(expo, axis=1, keepdims=True) + a * lsufx[rows, :]
        w0 = jnp.where(chosen, 0.0, expo).astype(BF)
        w1 = jnp.where(chosen, expo, 0.0).astype(BF)
        o = dot(w0, pkv[0, 1, :, lanes]) + dot(w1, pkv[1, 1, :, lanes]) + a * osufx[rows, :]
        return o.astype(BF), m, total

    def o_to_y(n, i):
        yy = lax.rem(y + i, NY)
        send(osend.at[n, yy], orecv.at[n, (-i) % NY], c_o, 1 + n, at_zy(z, yy))
        send(stsend.at[n], strecv.at[n, (-i) % NY], c_st, 1 + n, at_zy(z, yy))

    def blend(weights, parts):
        total = None
        for low in (False, True):
            pieces = []
            for w in weights:
                w = w[:, :64]
                high = w.astype(BF).astype(F32)
                w = w - high if low else high
                pieces.append(jnp.where(diagonal, jnp.broadcast_to(w, (64, 64)), 0.0).astype(BF))
            term = dot(jnp.concatenate(pieces, axis=1), jnp.concatenate(parts, axis=0))
            total = term if total is None else total + term
        return total

    odd_y = jnp.zeros((1, 128), jnp.int32) + lax.rem(y, 2) == 1
    stat_row = 2 * (y // 2)

    def merge(n):
        maxima, totals, parts = [], [], []
        landed(orecv.at[n, pl.ds(1, NY - 1)], c_o, 1 + n)
        landed(strecv.at[n, pl.ds(1, NY - 1)], c_st, 1 + n)
        for i in range(NY):
            if i:
                parts.append(orecv[n, i])
                m = strecv[n, i, pl.ds(stat_row, 1), :]
                total = strecv[n, i, pl.ds(stat_row + 1, 1), :]
            else:
                parts.append(osend[n, y])
                m = stsend[n, pl.ds(stat_row, 1), :]
                total = stsend[n, pl.ds(stat_row + 1, 1), :]
            maxima.append(jnp.where(odd_y, pltpu.roll(m, 64, 1), m))
            totals.append(jnp.where(odd_y, pltpu.roll(total, 64, 1), total))
        top = functools.reduce(jnp.maximum, maxima)
        weights = [jnp.exp(m - top) for m in maxima]
        total = sum(w * t for w, t in zip(weights, totals))
        ozsend[n] = blend(weights, parts).astype(BF)
        first = lax.broadcasted_iota(jnp.int32, (8, 128), 0) == 0
        stzsend[n] = jnp.where(
            first, jnp.broadcast_to(top, (8, 128)), jnp.broadcast_to(total, (8, 128))
        )
        if FAR[n]:
            there = at_zy(lax.rem(z + FAR[n], NZ), y)
            send(ozsend.at[n], ozrecv.at[n], c_oz, 1 + n, there)
            send(stzsend.at[n], stzrecv.at[n], c_stz, 1 + n, there)

    for n in range(NZ):
        zz = lax.rem(z + FAR[n], NZ)
        o0, m0, t0 = attend(2 * zz)
        o1, m1, t1 = attend(2 * zz + 1)
        for g in range(2):
            osend[n, g] = o0[g * 64 : (g + 1) * 64]
            osend[n, 2 + g] = o1[g * 64 : (g + 1) * 64]
        stats = jnp.where(
            lane == 0, m0, jnp.where(lane == 1, t0, jnp.where(lane == 2, m1, t1))
        )
        stsend[n] = stats.T[0:8]
        for i in Y_OFFSETS:
            o_to_y(n, i)
        if n >= LAG:
            merge(n - LAG)
    for n in range(NZ - LAG, NZ):
        merge(n)

    all_left(orecv.at[pl.ds(0, NZ), pl.ds(1, NY - 1)], c_o)
    all_left(strecv.at[pl.ds(0, NZ), pl.ds(1, NY - 1)], c_st)
    all_left(ozrecv.at[pl.ds(0, NZ - 1)], c_oz)
    all_left(stzrecv.at[pl.ds(0, NZ - 1)], c_stz)

    maxima, totals, parts = [], [], []
    for n in range(NZ - 1):
        landed(ozrecv.at[n], c_oz, 1 + n)
        landed(stzrecv.at[n], c_stz, 1 + n)
        maxima.append(stzrecv[n, 0:1, :])
        totals.append(stzrecv[n, 1:2, :])
        parts.append(ozrecv[n])
    maxima.append(stzsend[NZ - 1, 0:1, :])
    totals.append(stzsend[NZ - 1, 1:2, :])
    parts.append(ozsend[NZ - 1])
    top = functools.reduce(jnp.maximum, maxima)
    weights = [jnp.exp(m - top) for m in maxima]
    total = sum(w * t for w, t in zip(weights, totals))
    attended = blend([w / total for w in weights], parts).astype(BF)

    need(loads, 12)
    for j in range(CHUNKS // 2):
        r = dot(attended, wout[:, 256 * j : 256 * (j + 1)])
        for t in range(2):
            for s in range(2):
                pf[pl.ds(4 * j + 2 * t + s, NP, stride=PROJ_ROWS), :] = r[
                    s * 32 : (s + 1) * 32, t * 128 : (t + 1) * 128
                ]
    for s in range(2 * CHUNKS, PROJ_ROWS):
        pf[pl.ds(s, NP, stride=PROJ_ROWS), :] = jnp.zeros((NP, 128), F32)

    def reduced(n_z, y_out, y_in, z_out, z_in, sem_y, sem_z):
        def to_y(n, i):
            there = at_zy(z, lax.rem(y + i, NY))
            send(y_out.at[n, i], y_in.at[n, (-i) % NY], sem_y, 1 + n, there)

        def add_y(n):
            landed(y_in.at[n, pl.ds(1, NY - 1)], sem_y, 1 + n)
            total = y_out[n, 0].astype(F32)
            for i in Y_OFFSETS:
                total = total + y_in[n, i].astype(F32)
            return total

        def to_z(n, total):
            z_out[n] = total.astype(BF)
            there = at_zy(lax.rem(z + n_z[n], NZ), y)
            send(z_out.at[n], z_in.at[n], sem_z, 1 + n, there)

        def add_z(n):
            landed(z_in.at[n], sem_z, 1 + n)
            return z_in[n].astype(F32)

        all_left(y_in.at[pl.ds(0, NZ), pl.ds(1, NY - 1)], sem_y)
        all_left(z_in.at[pl.ds(0, NZ - 1)], sem_z)
        return to_y, add_y, to_z, add_z

    p_to_y, p_add_y, p_to_z, p_add_z = reduced(FAR, psend, precv, pzsend, pzrecv, d_y, d_z)
    for n in range(NZ):
        for i in Y_OFFSETS + (0,):
            o = lax.rem(z + FAR[n], NZ) * NY + lax.rem(y + i, NY)
            start = pl.multiple_of(o * PROJ_ROWS, 8)
            psend[n, i] = pf[pl.ds(start, PROJ_ROWS), :].astype(BF)
            if i:
                p_to_y(n, i)
    for n in (4, 5, 6):
        need(loads, n)
    for j in range(CHUNKS):
        cols = slice(j * 128, (j + 1) * 128)
        resid[2 * j : 2 * j + 2, :] = resid_ref[:, cols].astype(F32)
        gains[0, 2 * j : 2 * j + 2, :] = jnp.broadcast_to(again_ref[cols].reshape(1, 128), (2, 128))
        gains[1, 2 * j : 2 * j + 2, :] = jnp.broadcast_to(fgain_ref[cols].reshape(1, 128), (2, 128))
    for n in range(NZ - 1):
        p_to_z(n, p_add_y(n))
    projected = p_add_y(NZ - 1)
    for n in range(NZ - 1):
        projected = projected + p_add_z(n)

    row = lax.broadcasted_iota(jnp.int32, (PROJ_ROWS, 128), 0)
    odd = row % 2 == 1
    real = row < 2 * CHUNKS

    def normed(values, gain):
        square = jnp.where(real, values * values, 0.0)
        second = jnp.sum(jnp.where(odd, square, 0.0))
        first = jnp.sum(jnp.where(odd, 0.0, square))
        inv = jnp.where(odd, second, first) * (1.0 / D) + EPSILON
        return values * lax.rsqrt(inv) * gain

    midway = (resid[...] + normed(projected, gains[0])).astype(BF)
    settled = midway.astype(F32)
    ffn_in = normed(settled, gains[1]).astype(BF).astype(F32)
    ffn_in = jnp.where(real, ffn_in, 0.0)

    lane = lax.broadcasted_iota(jnp.int32, (12, 128), 1)
    rolled = [ffn_in if o == 0 else pltpu.roll(ffn_in, 128 - o, 1) for o in (0, 32, 64, 96)]
    for b in range(NS):
        o, j0 = 32 * (b % 4), (21 * b) // 4
        v = rolled[b % 4]
        piece = v[2 * j0 : 2 * j0 + 12]
        if o:
            piece = jnp.where(lane < 128 - o, piece, v[2 * j0 + 2 : 2 * j0 + 14])
        piece = jnp.concatenate([piece, jnp.zeros((4, 128), F32)], axis=0)
        e1send[b // NC, b % NC] = piece.astype(BF)

    for i in range(1, NS):
        b = lax.rem(spos + i, NS)
        send(e1send.at[b // NC], e1recv.at[spos], e_1, 1, at_sample(b))
    all_left(e1recv.at[pl.ds(1, NS - 1)], e_1)
    e1recv[spos] = e1send[x]
    for j in range(CHUNKS):
        mid_ref[:, j * 128 : (j + 1) * 128] = settled[2 * j : 2 * j + 2].astype(BF)
    mid_copy = pltpu.make_async_copy(mid_ref, mid_hbm, out_sem.at[0])
    mid_copy.start()
    ending.append(mid_copy.wait)
    landed(e1recv.at[pl.ds(1, NS - 1)], e_1, 1)
    for cc in range(NC):
        for b in range(NS):
            e1f[16 * b : 16 * (b + 1), :] = e1recv[b, cc].astype(F32)
        for i in range(6):
            for s in range(2):
                xf[i, pl.ds(s, 8, stride=2), :] = e1f[pl.ds(2 * i + s, 8, stride=16), :]
        for i in range(6):
            xown[cc, :, i * 128 : (i + 1) * 128] = xf[i].astype(BF)

    def turn(t):
        return FFN_ORDER[2 * t] * (1 - c) + FFN_ORDER[2 * t + 1] * c

    def x_to_z(t):
        send(xown, xall.at[t, 0], e_z, 1 + t, at_zy(lax.rem(z + NZ - turn(t), NZ), y))

    def x_to_y(t):
        for i in Y_OFFSETS:
            there = at_zy(z, lax.rem(y + i, NY))
            send(xall.at[t, 0], xall.at[t, (-i) % NY], e_y, 1 + t, there)

    for t in (3, 2, 1):
        x_to_z(t)

    @pl.when(c == 0)
    def _():
        xall[0, 0] = xown[...]

    @pl.when(c == 1)
    def _():
        x_to_z(0)
        landed(xall.at[0, 0], e_z, 1)

    x_to_y(0)
    for t in range(1, TURNS):
        landed(xall.at[t, 0], e_z, 1 + t)
        x_to_y(t)
    all_left(xall.at[pl.ds(0, TURNS), pl.ds(1, NY - 1)], e_y)

    def some_left(ref, sem):
        less = ref.at[pl.ds(1, ref.shape[0] - 1)]
        for cc, sent in ((0, less), (1, ref)):

            @pl.when(c == cc)
            def _(sent=sent):
                remote(sent, sent, sem.at[0], sem.at[0], at_xc(x, c)).wait_send()

    ending.append(lambda: some_left(xall.at[pl.ds(0, TURNS), 0], e_z))

    for t in range(3):
        need(loads, 13 + t)
        landed(ffw.at[t, 1 - c], w_c, 1 + t)

    def stage_a(t):
        landed(xall.at[t, pl.ds(1, NY - 1)], e_y, 1 + t)
        v = [xall[t, :, cc].reshape(64, 768)[:, :BLOCK] for cc in range(NC)]
        for n in range(2):
            part = dot(v[0], ffw[n, 0]) + dot(v[1], ffw[n, 1])
            gu[t, :, n] = part.astype(BF).reshape(NY, 16, BLOCK)
        for i in X_OFFSETS:
            xx = lax.rem(x + i, NX)
            send(gu.at[t, xx], gurecv.at[t, i], f_x, 1 + t, at_xc(xx, c))

    def stage_c(t):
        landed(gurecv.at[t, pl.ds(1, NX - 1)], f_x, 1 + t)
        total = gu[t, x].astype(F32)
        for i in X_OFFSETS:
            total = total + gurecv[t, i].astype(F32)
        own = hid.at[t, x]
        own[...] = (jax.nn.gelu(total[0], approximate=True) * total[1]).astype(BF)
        for i in X_OFFSETS:
            send(own, own, f_hx, 1 + t, at_xc(lax.rem(x + i, NX), c))

    def stage_e(t):
        landed(hid.at[t, pl.ds(0, NX - 1)], f_hx, 1 + t)
        hidden = hid[t].reshape(64, BLOCK)
        for cc in range(NC):
            ysend[t, :, cc] = dot(hidden, ffw[2, cc]).astype(BF).reshape(NY, 16, BLOCK)
        for i in Y_OFFSETS:
            there = at_zy(z, lax.rem(y + i, NY))
            send(ysend.at[t, i], yrecv.at[t, (-i) % NY], g_y, 1 + t, there)

    def stage_f(t):
        landed(yrecv.at[t, pl.ds(1, NY - 1)], g_y, 1 + t)
        total = ysend[t, 0].astype(F32)
        for i in Y_OFFSETS:
            total = total + yrecv[t, i].astype(F32)
        zsend[t] = total.astype(BF)
        zz = lax.rem(z + turn(t), NZ)
        n = 2 * t + c

        def to_core(cc):
            send(zsend.at[t, cc], zrecv.at[n], g_z, 1 + n, at_zyc(zz, y, cc))

        to_core(1)
        if t:
            to_core(0)
        else:

            @pl.when(c == 1)
            def _():
                to_core(0)

    all_left(gurecv.at[pl.ds(0, TURNS), pl.ds(1, NX - 1)], f_x)
    all_left(hid.at[pl.ds(0, TURNS), pl.ds(0, NX - 1)], f_hx)
    all_left(yrecv.at[pl.ds(0, TURNS), pl.ds(1, NY - 1)], g_y)
    ending.append(lambda: some_left(zrecv, g_z))
    stages = {"a": stage_a, "c": stage_c, "e": stage_e, "f": stage_f}
    for name, t in SCHEDULE:
        stages[name](t)

    @pl.when(c == 0)
    def _():
        zrecv[0] = zsend[0, 0]

    @pl.when(c == 1)
    def _():
        landed(zrecv.at[0], g_z, 1)

    total = zrecv[0].astype(F32)
    for n in range(1, NZ):
        landed(zrecv.at[n], g_z, 1 + n)
        total = total + zrecv[n].astype(F32)
    out_ref[...] = total.astype(BF)
    out_copy = pltpu.make_async_copy(out_ref, out_hbm, out_sem.at[1])
    out_copy.start()
    ending.append(out_copy.wait)


def local(
    residual,
    queries,
    fresh_key_value,
    prompt_key_value,
    suffix_key_value,
    suffix_len,
    sample_prompt,
    out_weight,
    attn_gain,
    ffn_gain,
    gate_weight,
    up_weight,
    down_weight,
):
    hbm = pl.BlockSpec(memory_space=pl.ANY)
    vmem = pl.BlockSpec(memory_space=pltpu.VMEM)
    V = pltpu.VMEM
    dma = pltpu.SemaphoreType.DMA
    scratch = [
        V((2, HEADS * WIDTH), BF),
        V((2, 2, KV * WIDTH), BF),
        V((2, D), BF),
        V((D,), F32),
        V((D,), F32),
        pltpu.SMEM((2,), jnp.int32),
        pltpu.SMEM((2 * NP * NS,), jnp.int32),
        V((2, D), BF),
        V((16, BLOCK), BF),
        dma((2,)),
        V((2, 2, 128, 2048), BF),
        V((2, 2, SUFX, 2048), BF),
        V((128, D), BF),
        V((3, NC, BLOCK, BLOCK), BF),
        dma((16,)),
        V((64, 128), F32),
        V((NZ, NY, 64, 128), BF),
        V((NP * 64, 128), F32),
        V((128, 128), F32),
        V((64, SUFX), F32),
        V((KV * 128, 128), F32),
        V((KV * 128, 128), F32),
        V((KV * 128, 128), F32),
        V((NZ, NY, 64, 128), BF),
        V((NZ, NY, 64, 128), BF),
        V((NZ, 8, 128), F32),
        V((NZ, NY, 8, 128), F32),
        V((NZ, 64, 128), BF),
        V((NZ, 64, 128), BF),
        V((NZ, 8, 128), F32),
        V((NZ, 8, 128), F32),
        V((NP * PROJ_ROWS, 128), F32),
        V((NZ, NY, PROJ_ROWS, 128), BF),
        V((NZ, NY, PROJ_ROWS, 128), BF),
        V((NZ, PROJ_ROWS, 128), BF),
        V((NZ, PROJ_ROWS, 128), BF),
        V((2, PROJ_ROWS, 128), F32),
        V((PROJ_ROWS, 128), F32),
        V((NX, NC, 16, 128), BF),
        V((NS, NC, 16, 128), BF),
        V((NS * 16, 128), F32),
        V((6, 16, 128), F32),
        V((NC, 16, 768), BF),
        V((TURNS, NY, NC, 16, 768), BF),
        V((TURNS, NX, 2, 16, BLOCK), BF),
        V((TURNS, NX, 2, 16, BLOCK), BF),
        V((TURNS, NX, 16, BLOCK), BF),
        V((TURNS, NY, NC, 16, BLOCK), BF),
        V((TURNS, NY, NC, 16, BLOCK), BF),
        V((TURNS, NC, 16, BLOCK), BF),
        V((NZ, 16, BLOCK), BF),
        dma((4,)),
        dma((1 + NZ,)),
        dma((1 + NZ,)),
        dma((1 + NZ,)),
        dma((1 + NZ,)),
        dma((1 + NZ,)),
        dma((1 + NZ,)),
        dma((1 + NZ,)),
        dma((1 + NZ,)),
        dma((2,)),
        dma((1 + TURNS,)),
        dma((1 + TURNS,)),
        dma((1 + TURNS,)),
        dma((1 + TURNS,)),
        dma((1 + TURNS,)),
        dma((1 + NZ,)),
    ]
    outs = pl.pallas_call(
        body,
        out_shape=(
            jax.ShapeDtypeStruct((2, D), BF),
            jax.ShapeDtypeStruct((16, BLOCK), BF),
        ),
        in_specs=[hbm] * 13,
        out_specs=(hbm, hbm),
        scratch_shapes=scratch,
        compiler_params=pltpu.CompilerParams(
            collective_id=0, has_side_effects=True, vmem_limit_bytes=56 << 20
        ),
        name="layer",
    )(
        queries,
        fresh_key_value,
        residual,
        attn_gain,
        ffn_gain,
        suffix_len,
        sample_prompt,
        prompt_key_value,
        suffix_key_value,
        out_weight,
        gate_weight,
        up_weight,
        down_weight,
    )
    return pl.pallas_call(
        hand_over,
        out_shape=tuple(jax.ShapeDtypeStruct(v.shape, v.dtype) for v in outs),
        in_specs=[vmem, vmem],
        out_specs=(vmem, vmem),
        name="hand_over",
    )(*outs)


def hand_over(mid, out, mid_to, out_to):
    mid_to[...] = mid[...]
    out_to[...] = out[...]


def solution(mesh):
    return jax.shard_map(
        local,
        mesh=mesh,
        in_specs=(
            P(("prefix", "sample"), None),
            P(("prefix", "sample"), None),
            P(("prefix", "sample"), None, None),
            P("sample", None, "prefix", None),
            P(("prefix", "sample"), None, None, None),
            P(("prefix", "sample")),
            P(),
            P("prefix", None),
            P(),
            P(),
            P("sample", "prefix"),
            P("sample", "prefix"),
            P("prefix", "sample"),
        ),
        out_specs=(P(("prefix", "sample"), None), P("prefix", "sample")),
        check_vma=False,
    )
```

```python
import functools

import jax
import jax.numpy as jnp
from jax import lax
from jax.experimental import pallas as pl
from jax.experimental.pallas import tpu as pltpu
from jax.sharding import PartitionSpec as P

MESH = pl.DeviceIdType.MESH
SCALE = 168.0 ** (-0.5)
NEGATIVE = -1e30
EPSILON = 1e-06
BF = jnp.bfloat16
F32 = jnp.float32

NZ, NY, NX, NC = 8, 4, 4, 2
NP, NS = NZ * NY, NX * NC
HEADS, KV, WIDTH = 32, 16, 128
D = 5376
CHUNKS = D // 128
PROJ_ROWS = 88
MAIN_ROWS = 72
MAIN = 544
BLOCK = 672
SUF = 192
SUFX = 208
Y_OFFSETS = X_OFFSETS = (1, 3, 2)
LAG = 6
NEAR = (0, 1, 7, 2, 6, 3, 5, 4)
FFN_ORDER = (0, 1, 4, 7, 2, 6, 5, 3)
FAR = (4, 5, 3, 6, 2, 7, 1, 0)
TURNS = 4
SCHEDULE = (
    ("a", 0), ("a", 1), ("a", 2), ("a", 3),
    ("c", 0), ("c", 1), ("c", 2), ("c", 3),
    ("e", 0), ("e", 1), ("e", 2), ("e", 3),
    ("f", 0), ("f", 1), ("f", 2), ("f", 3),
)


def dot(a, b):
    return jnp.dot(a, b, preferred_element_type=F32)


def dot_t(a, b):
    return lax.dot_general(a, b, (((1,), (1,)), ((), ())), preferred_element_type=F32)


def remote(src, dst, send_sem, recv_sem, device):
    return pltpu.make_async_remote_copy(
        src_ref=src,
        dst_ref=dst,
        send_sem=send_sem,
        recv_sem=recv_sem,
        device_id=device,
        device_id_type=MESH,
    )


def need(loads, n):
    loads[n].wait()


def body(*refs):
    ending, loads = [], []
    layer(ending, loads, *refs)
    for wait in ending:
        wait()


def layer(
    ending,
    loads,
    q_hbm,
    fresh_hbm,
    resid_hbm,
    again_hbm,
    fgain_hbm,
    slen_hbm,
    sprompt_hbm,
    pkv_hbm,
    skv_hbm,
    wout_hbm,
    wg_hbm,
    wu_hbm,
    wd_hbm,
    mid_hbm,
    out_hbm,
    q_ref,
    fresh_ref,
    resid_ref,
    again_ref,
    fgain_ref,
    slen_ref,
    sprompt_ref,
    mid_ref,
    out_ref,
    out_sem,
    pkv,
    skv,
    wout,
    ffw,
    load_sem,
    q32,
    qall,
    qflat,
    sel,
    ssuf,
    msufx,
    lsufx,
    osufx,
    osend,
    orecv,
    stsend,
    strecv,
    ozsend,
    ozrecv,
    stzsend,
    stzrecv,
    pf,
    psend,
    precv,
    pzsend,
    pzrecv,
    pbsend,
    pbrecv,
    pby,
    pbyrecv,
    gains,
    resid,
    e1send,
    e1recv,
    e1f,
    xf,
    xown,
    xall,
    xby,
    xallb,
    gu,
    gurecv,
    hid,
    ysend,
    yrecv,
    zsend,
    zrecv,
    ybsend,
    zbrecv,
    yby,
    ybyrecv,
    w_c,
    aq_z,
    aq_y,
    c_o,
    c_st,
    c_oz,
    c_stz,
    d_y,
    d_z,
    d_bz,
    d_by,
    e_1,
    e_z,
    e_y,
    e_by,
    e_bz,
    f_x,
    f_hx,
    g_y,
    g_z,
    g_bz,
    g_by,
):
    me = lax.axis_index("prefix")
    spos = lax.axis_index("sample")
    z, y = me // NY, me % NY
    x, c = spos // NC, spos % NC

    def send(src, dst, sem, recv, device):
        remote(src, dst, sem.at[0], sem.at[recv], device).start()

    def all_left(ref, sem):
        ending.append(remote(ref, ref, sem.at[0], sem.at[0], at_xc(x, c)).wait_send)

    def landed(ref, sem, recv):
        remote(ref, ref, sem.at[0], sem.at[recv], at_xc(x, c)).wait_recv()

    def at_zy(zz, yy):
        return {"prefix": zz * NY + yy, "sample": spos}

    def at_zyc(zz, yy, cc):
        return {"prefix": zz * NY + yy, "sample": x * NC + cc}

    def at_sample(s):
        return {"prefix": me, "sample": s}

    def at_xc(xx, cc):
        return {"prefix": me, "sample": xx * NC + cc}

    barrier = pltpu.get_barrier_semaphore()

    for i in range(1, NZ):
        for cc in range(NC):
            there = at_zyc(lax.rem(z + i, NZ), y, cc)
            pl.semaphore_signal(barrier, 1, device_id=there, device_id_type=MESH)
    for i in range(1, NY):
        pl.semaphore_signal(
            barrier, 1, device_id=at_zy(z, lax.rem(y + i, NY)), device_id_type=MESH
        )

    @pl.loop(1, NS)
    def _(i):
        pl.semaphore_signal(
            barrier, 1, device_id=at_sample(lax.rem(spos + i, NS)), device_id_type=MESH
        )

    def load(src, dst):
        cp = pltpu.make_async_copy(src, dst, load_sem.at[len(loads)])
        cp.start()
        loads.append(cp)

    load(q_hbm, q_ref)
    load(sprompt_hbm, sprompt_ref)
    load(slen_hbm, slen_ref)
    load(fresh_hbm, fresh_ref)
    load(resid_hbm, resid_ref)
    load(again_hbm, again_ref)
    load(fgain_hbm, fgain_ref)
    for t in range(2):
        for s in range(2):
            load(skv_hbm.at[s, t], skv.at[s, t, pl.ds(0, SUF)])
    load(pkv_hbm, pkv)

    need(loads, 0)
    for h in range(HEADS):
        q32[2 * h : 2 * h + 2, :] = q_ref[:, h * 128 : (h + 1) * 128].astype(F32)
    qall[0, 0] = q32[...].astype(BF)

    pl.semaphore_wait(barrier, NC * (NZ - 1) + NY - 1 + NS - 1)

    def spread(order, buf, sem_z, sem_y):
        def to_y(n):
            for i in Y_OFFSETS:
                there = at_zy(z, lax.rem(y + i, NY))
                send(buf.at[n, 0], buf.at[n, (-i) % NY], sem_y, 1 + n, there)

        def start():
            for n in range(NZ - 1, 0, -1):
                slot = order.index((-order[n]) % NZ)
                there = at_zy(lax.rem(z + order[n], NZ), y)
                send(buf.at[0, 0], buf.at[slot, 0], sem_z, 1 + slot, there)
            to_y(0)
            all_left(buf.at[pl.ds(1, NZ - 1), 0], sem_z)
            all_left(buf.at[pl.ds(0, NZ), pl.ds(1, NY - 1)], sem_y)

        def pass_on(n):
            landed(buf.at[n, 0], sem_z, 1 + n)
            to_y(n)

        def take(n):
            landed(buf.at[n, pl.ds(1, NY - 1)], sem_y, 1 + n)

        return start, pass_on, take

    q_start, q_pass, q_take = spread(NEAR, qall, aq_z, aq_y)
    q_start()

    need(loads, 1)
    @pl.loop(0, 2 * NP)
    def _(r):
        value = sprompt_ref[lax.rem(r, NP) * 16 + 2 * spos + r // NP] - 2 * spos
        row = jnp.full((1, 128), value, jnp.int32).astype(F32)
        sel[pl.ds(r, 1), :] = row
        sel[pl.ds(r + 2 * NP, 1), :] = row

    msufx[...] = jnp.full(msufx.shape, NEGATIVE, F32)
    q_pass(1)

    need(loads, 3)
    first_row = lax.broadcasted_iota(jnp.int32, (16, 2048), 0) == 0
    for s in range(2):
        for t in range(2):
            row = jnp.broadcast_to(fresh_ref[s, t : t + 1, :].astype(F32), (16, 2048))
            skv[s, t, SUF:SUFX, :] = jnp.where(first_row, row, 0.0).astype(BF)
    q_pass(2)
    for s in range(2):
        need(loads, 7 + s)

    def suffix_scores(k):
        lanes = slice(k * 128, (k + 1) * 128)
        rows = q32[4 * k : 4 * k + 4, :].astype(BF)
        odd = lax.broadcasted_iota(jnp.int32, (4, SUFX), 0) % 2 == 1
        ssuf[4 * k : 4 * k + 4, :] = jnp.where(
            odd, dot_t(rows, skv[1, 0, :, lanes]), dot_t(rows, skv[0, 0, :, lanes])
        )

    for k in range(KV // 2):
        suffix_scores(k)
    q_pass(3)
    for k in range(KV // 2, KV):
        suffix_scores(k)
    q_pass(4)
    odd = lax.broadcasted_iota(jnp.int32, (64, SUFX), 0) % 2 == 1
    slot = lax.broadcasted_iota(jnp.int32, (64, SUFX), 1)
    need(loads, 2)
    length = jnp.where(odd, slen_ref[1], slen_ref[0])
    scores = jnp.where((slot < length) | (slot == SUF), ssuf[...] * SCALE, NEGATIVE)
    msuf = jnp.max(scores, axis=1, keepdims=True)
    expo = jnp.exp(scores - msuf)
    lsuf = jnp.broadcast_to(jnp.sum(expo, axis=1, keepdims=True), (64, 128))
    msuf = jnp.broadcast_to(msuf, (64, 128))
    even_w = jnp.where(odd, 0.0, expo)
    odd_w = jnp.where(odd, expo, 0.0)
    q_pass(5)
    q_pass(6)
    q_pass(7)
    lsufx[...] = jnp.zeros(lsufx.shape, F32)
    osufx[...] = jnp.zeros(osufx.shape, F32)
    for s in range(2):
        need(loads, 9 + s)
    for k in range(KV):
        lanes = slice(k * 128, (k + 1) * 128)
        part = slice(4 * k, 4 * k + 4)
        o = dot(even_w[part].astype(BF), skv[0, 1, :, lanes]) + dot(
            odd_w[part].astype(BF), skv[1, 1, :, lanes]
        )
        for g in range(2):
            for s in range(2):
                src = 4 * k + 2 * g + s
                dst = k * 128 + g * 64 + s * 32 + me
                msufx[pl.ds(dst, 1), :] = msuf[src : src + 1]
                lsufx[pl.ds(dst, 1), :] = lsuf[src : src + 1]
                osufx[pl.ds(dst, 1), :] = o[2 * g + s : 2 * g + s + 1]

    for n in range(NZ):
        q_take(n)
        for i in range(NY):
            owner = lax.rem(z + NEAR[n], NZ) * NY + lax.rem(y + i, NY)
            qflat[pl.ds(pl.multiple_of(owner * 64, 64), 64), :] = qall[n, i].astype(F32)

    load(wout_hbm, wout)
    for t, ref in enumerate((wg_hbm, wu_hbm, wd_hbm)):
        load(ref, ffw.at[t, c])
        send(ref, ffw.at[t, c], w_c, 1 + t, at_xc(x, 1 - c))
    all_left(ffw.at[pl.ds(0, 3), 0], w_c)

    need(loads, 11)
    chosen = sel[...] > 0.5
    lane = lax.broadcasted_iota(jnp.int32, (128, 128), 1)
    diagonal = lax.broadcasted_iota(jnp.int32, (64, 64), 0) == lax.broadcasted_iota(
        jnp.int32, (64, 64), 1
    )

    def attend(k):
        lanes = pl.ds(pl.multiple_of(k * 128, 128), 128)
        rows = pl.ds(pl.multiple_of(k * 128, 128), 128)
        q = jnp.concatenate(
            [qflat[pl.ds(4 * k + t, 32, stride=64), :] for t in range(4)], axis=0
        ).astype(BF)
        scores = jnp.where(chosen, dot_t(q, pkv[1, 0, :, lanes]), dot_t(q, pkv[0, 0, :, lanes]))
        scores = scores * SCALE
        ms = msufx[rows, :]
        m = jnp.maximum(ms, jnp.max(scores, axis=1, keepdims=True))
        expo = jnp.exp(scores - m)
        a = jnp.exp(ms - m)
        total = jnp.sum(expo, axis=1, keepdims=True) + a * lsufx[rows, :]
        w0 = jnp.where(chosen, 0.0, expo).astype(BF)
        w1 = jnp.where(chosen, expo, 0.0).astype(BF)
        o = dot(w0, pkv[0, 1, :, lanes]) + dot(w1, pkv[1, 1, :, lanes]) + a * osufx[rows, :]
        return o.astype(BF), m, total

    def o_to_y(n, i):
        yy = lax.rem(y + i, NY)
        send(osend.at[n, yy], orecv.at[n, (-i) % NY], c_o, 1 + n, at_zy(z, yy))
        send(stsend.at[n], strecv.at[n, (-i) % NY], c_st, 1 + n, at_zy(z, yy))

    def blend(weights, parts):
        total = None
        for low in (False, True):
            pieces = []
            for w in weights:
                w = w[:, :64]
                high = w.astype(BF).astype(F32)
                w = w - high if low else high
                pieces.append(jnp.where(diagonal, jnp.broadcast_to(w, (64, 64)), 0.0).astype(BF))
            term = dot(jnp.concatenate(pieces, axis=1), jnp.concatenate(parts, axis=0))
            total = term if total is None else total + term
        return total

    odd_y = jnp.zeros((1, 128), jnp.int32) + lax.rem(y, 2) == 1
    stat_row = 2 * (y // 2)

    def merge(n):
        maxima, totals, parts = [], [], []
        landed(orecv.at[n, pl.ds(1, NY - 1)], c_o, 1 + n)
        landed(strecv.at[n, pl.ds(1, NY - 1)], c_st, 1 + n)
        for i in range(NY):
            if i:
                parts.append(orecv[n, i])
                m = strecv[n, i, pl.ds(stat_row, 1), :]
                total = strecv[n, i, pl.ds(stat_row + 1, 1), :]
            else:
                parts.append(osend[n, y])
                m = stsend[n, pl.ds(stat_row, 1), :]
                total = stsend[n, pl.ds(stat_row + 1, 1), :]
            maxima.append(jnp.where(odd_y, pltpu.roll(m, 64, 1), m))
            totals.append(jnp.where(odd_y, pltpu.roll(total, 64, 1), total))
        top = functools.reduce(jnp.maximum, maxima)
        weights = [jnp.exp(m - top) for m in maxima]
        total = sum(w * t for w, t in zip(weights, totals))
        ozsend[n] = blend(weights, parts).astype(BF)
        first = lax.broadcasted_iota(jnp.int32, (8, 128), 0) == 0
        stzsend[n] = jnp.where(
            first, jnp.broadcast_to(top, (8, 128)), jnp.broadcast_to(total, (8, 128))
        )
        if FAR[n]:
            there = at_zy(lax.rem(z + FAR[n], NZ), y)
            send(ozsend.at[n], ozrecv.at[n], c_oz, 1 + n, there)
            send(stzsend.at[n], stzrecv.at[n], c_stz, 1 + n, there)

    for n in range(NZ):
        zz = lax.rem(z + FAR[n], NZ)
        o0, m0, t0 = attend(2 * zz)
        o1, m1, t1 = attend(2 * zz + 1)
        for g in range(2):
            osend[n, g] = o0[g * 64 : (g + 1) * 64]
            osend[n, 2 + g] = o1[g * 64 : (g + 1) * 64]
        stats = jnp.where(
            lane == 0, m0, jnp.where(lane == 1, t0, jnp.where(lane == 2, m1, t1))
        )
        stsend[n] = stats.T[0:8]
        for i in Y_OFFSETS:
            o_to_y(n, i)
        if n >= LAG:
            merge(n - LAG)
    for n in range(NZ - LAG, NZ):
        merge(n)

    all_left(orecv.at[pl.ds(0, NZ), pl.ds(1, NY - 1)], c_o)
    all_left(strecv.at[pl.ds(0, NZ), pl.ds(1, NY - 1)], c_st)
    all_left(ozrecv.at[pl.ds(0, NZ - 1)], c_oz)
    all_left(stzrecv.at[pl.ds(0, NZ - 1)], c_stz)

    maxima, totals, parts = [], [], []
    for n in range(NZ - 1):
        landed(ozrecv.at[n], c_oz, 1 + n)
        landed(stzrecv.at[n], c_stz, 1 + n)
        maxima.append(stzrecv[n, 0:1, :])
        totals.append(stzrecv[n, 1:2, :])
        parts.append(ozrecv[n])
    maxima.append(stzsend[NZ - 1, 0:1, :])
    totals.append(stzsend[NZ - 1, 1:2, :])
    parts.append(ozsend[NZ - 1])
    top = functools.reduce(jnp.maximum, maxima)
    weights = [jnp.exp(m - top) for m in maxima]
    total = sum(w * t for w, t in zip(weights, totals))
    attended = blend([w / total for w in weights], parts).astype(BF)

    need(loads, 12)
    for j in range(CHUNKS // 2):
        r = dot(attended, wout[:, 256 * j : 256 * (j + 1)])
        for t in range(2):
            for s in range(2):
                pf[pl.ds(4 * j + 2 * t + s, NP, stride=PROJ_ROWS), :] = r[
                    s * 32 : (s + 1) * 32, t * 128 : (t + 1) * 128
                ]
    for s in range(2 * CHUNKS, PROJ_ROWS):
        pf[pl.ds(s, NP, stride=PROJ_ROWS), :] = jnp.zeros((NP, 128), F32)

    def reduced(n_z, y_out, y_in, z_out, z_in, sem_y, sem_z):
        def to_y(n, i):
            there = at_zy(z, lax.rem(y + i, NY))
            send(y_out.at[n, i], y_in.at[n, (-i) % NY], sem_y, 1 + n, there)

        def add_y(n):
            landed(y_in.at[n, pl.ds(1, NY - 1)], sem_y, 1 + n)
            total = y_out[n, 0].astype(F32)
            for i in Y_OFFSETS:
                total = total + y_in[n, i].astype(F32)
            return total

        def to_z(n, total):
            z_out[n] = total.astype(BF)
            there = at_zy(lax.rem(z + n_z[n], NZ), y)
            send(z_out.at[n], z_in.at[n], sem_z, 1 + n, there)

        def add_z(n):
            landed(z_in.at[n], sem_z, 1 + n)
            return z_in[n].astype(F32)

        all_left(y_in.at[pl.ds(0, NZ), pl.ds(1, NY - 1)], sem_y)
        all_left(z_in.at[pl.ds(0, NZ - 1)], sem_z)
        return to_y, add_y, to_z, add_z

    p_to_y, p_add_y, p_to_z, p_add_z = reduced(FAR, psend, precv, pzsend, pzrecv, d_y, d_z)
    for n in range(NZ):
        for i in Y_OFFSETS + (0,):
            o = lax.rem(z + FAR[n], NZ) * NY + lax.rem(y + i, NY)
            start = pl.multiple_of(o * PROJ_ROWS, 8)
            start_b = pl.multiple_of(o * PROJ_ROWS + MAIN_ROWS, 8)
            psend[n, i] = pf[pl.ds(start, MAIN_ROWS), :].astype(BF)
            pbsend[n, i] = pf[pl.ds(start_b, PROJ_ROWS - MAIN_ROWS), :].astype(BF)
            if i:
                p_to_y(n, i)
        if FAR[n]:
            there = at_zy(lax.rem(z + FAR[n], NZ), y)
            send(pbsend.at[n], pbrecv.at[n], d_bz, 1 + n, there)
    all_left(pbrecv.at[pl.ds(0, NZ - 1)], d_bz)
    for n in (4, 5, 6):
        need(loads, n)
    for j in range(CHUNKS):
        cols = slice(j * 128, (j + 1) * 128)
        resid[2 * j : 2 * j + 2, :] = resid_ref[:, cols].astype(F32)
        gains[0, 2 * j : 2 * j + 2, :] = jnp.broadcast_to(again_ref[cols].reshape(1, 128), (2, 128))
        gains[1, 2 * j : 2 * j + 2, :] = jnp.broadcast_to(fgain_ref[cols].reshape(1, 128), (2, 128))
    for n in range(NZ - 1):
        p_to_z(n, p_add_y(n))
    rest = pbsend[NZ - 1].astype(F32)
    for n in range(NZ - 1):
        landed(pbrecv.at[n], d_bz, 1 + n)
        rest = rest + pbrecv[n].astype(F32)
    pby[...] = rest.astype(BF)
    for i in Y_OFFSETS:
        send(pby.at[i], pbyrecv.at[(-i) % NY], d_by, 1, at_zy(z, lax.rem(y + i, NY)))
    all_left(pbyrecv.at[pl.ds(1, NY - 1)], d_by)
    projected = p_add_y(NZ - 1)
    for n in range(NZ - 1):
        projected = projected + p_add_z(n)
    landed(pbyrecv.at[pl.ds(1, NY - 1)], d_by, 1)
    rest = pby[0].astype(F32)
    for i in Y_OFFSETS:
        rest = rest + pbyrecv[i].astype(F32)
    projected = jnp.concatenate([projected, rest], axis=0)

    row = lax.broadcasted_iota(jnp.int32, (PROJ_ROWS, 128), 0)
    odd = row % 2 == 1
    real = row < 2 * CHUNKS

    def normed(values, gain):
        square = jnp.where(real, values * values, 0.0)
        second = jnp.sum(jnp.where(odd, square, 0.0))
        first = jnp.sum(jnp.where(odd, 0.0, square))
        inv = jnp.where(odd, second, first) * (1.0 / D) + EPSILON
        return values * lax.rsqrt(inv) * gain

    midway = (resid[...] + normed(projected, gains[0])).astype(BF)
    settled = midway.astype(F32)
    ffn_in = normed(settled, gains[1]).astype(BF).astype(F32)
    ffn_in = jnp.where(real, ffn_in, 0.0)

    lane = lax.broadcasted_iota(jnp.int32, (12, 128), 1)
    rolled = [ffn_in if o == 0 else pltpu.roll(ffn_in, 128 - o, 1) for o in (0, 32, 64, 96)]
    for b in range(NS):
        o, j0 = 32 * (b % 4), (21 * b) // 4
        v = rolled[b % 4]
        piece = v[2 * j0 : 2 * j0 + 12]
        if o:
            piece = jnp.where(lane < 128 - o, piece, v[2 * j0 + 2 : 2 * j0 + 14])
        piece = jnp.concatenate([piece, jnp.zeros((4, 128), F32)], axis=0)
        e1send[b // NC, b % NC] = piece.astype(BF)

    for i in range(1, NS):
        b = lax.rem(spos + i, NS)
        send(e1send.at[b // NC], e1recv.at[spos], e_1, 1, at_sample(b))
    all_left(e1recv.at[pl.ds(1, NS - 1)], e_1)
    e1recv[spos] = e1send[x]
    for j in range(CHUNKS):
        mid_ref[:, j * 128 : (j + 1) * 128] = settled[2 * j : 2 * j + 2].astype(BF)
    mid_copy = pltpu.make_async_copy(mid_ref, mid_hbm, out_sem.at[0])
    mid_copy.start()
    ending.append(mid_copy.wait)
    landed(e1recv.at[pl.ds(1, NS - 1)], e_1, 1)
    for cc in range(NC):
        for b in range(NS):
            e1f[16 * b : 16 * (b + 1), :] = e1recv[b, cc].astype(F32)
        for i in range(6):
            for s in range(2):
                xf[i, pl.ds(s, 8, stride=2), :] = e1f[pl.ds(2 * i + s, 8, stride=16), :]
        xby[0, cc] = xf[0].astype(BF)
        for i in range(1, 6):
            xown[cc, :, (i - 1) * 128 : i * 128] = xf[i].astype(BF)

    def turn(t):
        return FFN_ORDER[2 * t] * (1 - c) + FFN_ORDER[2 * t + 1] * c

    def x_to_z(t):
        send(xown, xall.at[t, 0], e_z, 1 + t, at_zy(lax.rem(z + NZ - turn(t), NZ), y))

    def x_to_y(t):
        for i in Y_OFFSETS:
            there = at_zy(z, lax.rem(y + i, NY))
            send(xall.at[t, 0], xall.at[t, (-i) % NY], e_y, 1 + t, there)

    for i in Y_OFFSETS:
        send(xby.at[0], xby.at[(-i) % NY], e_by, 1, at_zy(z, lax.rem(y + i, NY)))
    all_left(xby.at[pl.ds(1, NY - 1)], e_by)

    def xb_to_z(t):
        send(xby, xallb.at[t], e_bz, 1 + t, at_zy(lax.rem(z + NZ - turn(t), NZ), y))

    for t in (3, 2, 1):
        x_to_z(t)

    @pl.when(c == 0)
    def _():
        xall[0, 0] = xown[...]

    @pl.when(c == 1)
    def _():
        x_to_z(0)
        landed(xall.at[0, 0], e_z, 1)

    x_to_y(0)
    landed(xby.at[pl.ds(1, NY - 1)], e_by, 1)
    for t in (3, 2, 1):
        xb_to_z(t)

    @pl.when(c == 0)
    def _():
        xallb[0] = xby[...]

    @pl.when(c == 1)
    def _():
        xb_to_z(0)

    for t in range(1, TURNS):
        landed(xall.at[t, 0], e_z, 1 + t)
        x_to_y(t)
    all_left(xall.at[pl.ds(0, TURNS), pl.ds(1, NY - 1)], e_y)

    def some_left(ref, sem):
        less = ref.at[pl.ds(1, ref.shape[0] - 1)]
        for cc, sent in ((0, less), (1, ref)):

            @pl.when(c == cc)
            def _(sent=sent):
                remote(sent, sent, sem.at[0], sem.at[0], at_xc(x, c)).wait_send()

    ending.append(lambda: some_left(xall.at[pl.ds(0, TURNS), 0], e_z))
    ending.append(lambda: some_left(xallb, e_bz))

    for t in range(3):
        need(loads, 13 + t)
        landed(ffw.at[t, 1 - c], w_c, 1 + t)

    def stage_a(t):
        landed(xall.at[t, pl.ds(1, NY - 1)], e_y, 1 + t)
        if t:
            landed(xallb.at[t], e_bz, 1 + t)
        else:

            @pl.when(c == 1)
            def _():
                landed(xallb.at[0], e_bz, 1)

        v = []
        for cc in range(NC):
            main = xall[t, :, cc].reshape(64, 640)[:, :MAIN]
            v.append(jnp.concatenate([xallb[t, :, cc].reshape(64, 128), main], axis=1))
        for n in range(2):
            part = dot(v[0], ffw[n, 0]) + dot(v[1], ffw[n, 1])
            gu[t, :, n] = part.astype(BF).reshape(NY, 16, BLOCK)
        for i in X_OFFSETS:
            xx = lax.rem(x + i, NX)
            send(gu.at[t, xx], gurecv.at[t, i], f_x, 1 + t, at_xc(xx, c))

    def stage_c(t):
        landed(gurecv.at[t, pl.ds(1, NX - 1)], f_x, 1 + t)
        total = gu[t, x].astype(F32)
        for i in X_OFFSETS:
            total = total + gurecv[t, i].astype(F32)
        own = hid.at[t, x]
        own[...] = (jax.nn.gelu(total[0], approximate=True) * total[1]).astype(BF)
        for i in X_OFFSETS:
            send(own, own, f_hx, 1 + t, at_xc(lax.rem(x + i, NX), c))

    def stage_e(t):
        landed(hid.at[t, pl.ds(0, NX - 1)], f_hx, 1 + t)
        hidden = hid[t].reshape(64, BLOCK)
        for cc in range(NC):
            down = dot(hidden, ffw[2, cc]).astype(BF)
            ybsend[t, cc] = down[:, :128].reshape(NY, 16, 128)
            ysend[t, :, cc] = down[:, 128:].reshape(NY, 16, MAIN)
        for i in Y_OFFSETS:
            there = at_zy(z, lax.rem(y + i, NY))
            send(ysend.at[t, i], yrecv.at[t, (-i) % NY], g_y, 1 + t, there)
        to_cores(t, lambda n, cc, there: send(ybsend.at[t, cc], zbrecv.at[n], g_bz, 1 + n, there))

    def to_cores(t, send_one):
        zz = lax.rem(z + turn(t), NZ)
        n = 2 * t + c
        send_one(n, 1, at_zyc(zz, y, 1))
        if t:
            send_one(n, 0, at_zyc(zz, y, 0))
        else:

            @pl.when(c == 1)
            def _():
                send_one(n, 0, at_zyc(zz, y, 0))

    def stage_f(t):
        landed(yrecv.at[t, pl.ds(1, NY - 1)], g_y, 1 + t)
        total = ysend[t, 0].astype(F32)
        for i in Y_OFFSETS:
            total = total + yrecv[t, i].astype(F32)
        zsend[t] = total.astype(BF)
        to_cores(t, lambda n, cc, there: send(zsend.at[t, cc], zrecv.at[n], g_z, 1 + n, there))

    all_left(gurecv.at[pl.ds(0, TURNS), pl.ds(1, NX - 1)], f_x)
    all_left(hid.at[pl.ds(0, TURNS), pl.ds(0, NX - 1)], f_hx)
    all_left(yrecv.at[pl.ds(0, TURNS), pl.ds(1, NY - 1)], g_y)
    stages = {"a": stage_a, "c": stage_c, "e": stage_e, "f": stage_f}
    for name, t in SCHEDULE:
        stages[name](t)

    def over_z(recv, own, sem):
        @pl.when(c == 0)
        def _():
            recv[0] = own[...]

        @pl.when(c == 1)
        def _():
            landed(recv.at[0], sem, 1)

        total = recv[0].astype(F32)
        for n in range(1, NZ):
            landed(recv.at[n], sem, 1 + n)
            total = total + recv[n].astype(F32)
        ending.append(lambda: some_left(recv, sem))
        return total

    yby[...] = over_z(zbrecv, ybsend.at[0, 0], g_bz).astype(BF)
    for i in Y_OFFSETS:
        send(yby.at[i], ybyrecv.at[(-i) % NY], g_by, 1, at_zy(z, lax.rem(y + i, NY)))
    all_left(ybyrecv.at[pl.ds(1, NY - 1)], g_by)
    out_ref[:, 128:] = over_z(zrecv, zsend.at[0, 0], g_z).astype(BF)
    landed(ybyrecv.at[pl.ds(1, NY - 1)], g_by, 1)
    rest = yby[0].astype(F32)
    for i in Y_OFFSETS:
        rest = rest + ybyrecv[i].astype(F32)
    out_ref[:, :128] = rest.astype(BF)
    out_copy = pltpu.make_async_copy(out_ref, out_hbm, out_sem.at[1])
    out_copy.start()
    ending.append(out_copy.wait)


def local(
    residual,
    queries,
    fresh_key_value,
    prompt_key_value,
    suffix_key_value,
    suffix_len,
    sample_prompt,
    out_weight,
    attn_gain,
    ffn_gain,
    gate_weight,
    up_weight,
    down_weight,
):
    hbm = pl.BlockSpec(memory_space=pl.ANY)
    vmem = pl.BlockSpec(memory_space=pltpu.VMEM)
    V = pltpu.VMEM
    dma = pltpu.SemaphoreType.DMA
    scratch = [
        V((2, HEADS * WIDTH), BF),
        V((2, 2, KV * WIDTH), BF),
        V((2, D), BF),
        V((D,), F32),
        V((D,), F32),
        pltpu.SMEM((2,), jnp.int32),
        pltpu.SMEM((2 * NP * NS,), jnp.int32),
        V((2, D), BF),
        V((16, BLOCK), BF),
        dma((2,)),
        V((2, 2, 128, 2048), BF),
        V((2, 2, SUFX, 2048), BF),
        V((128, D), BF),
        V((3, NC, BLOCK, BLOCK), BF),
        dma((16,)),
        V((64, 128), F32),
        V((NZ, NY, 64, 128), BF),
        V((NP * 64, 128), F32),
        V((128, 128), F32),
        V((64, SUFX), F32),
        V((KV * 128, 128), F32),
        V((KV * 128, 128), F32),
        V((KV * 128, 128), F32),
        V((NZ, NY, 64, 128), BF),
        V((NZ, NY, 64, 128), BF),
        V((NZ, 8, 128), F32),
        V((NZ, NY, 8, 128), F32),
        V((NZ, 64, 128), BF),
        V((NZ, 64, 128), BF),
        V((NZ, 8, 128), F32),
        V((NZ, 8, 128), F32),
        V((NP * PROJ_ROWS, 128), F32),
        V((NZ, NY, MAIN_ROWS, 128), BF),
        V((NZ, NY, MAIN_ROWS, 128), BF),
        V((NZ, MAIN_ROWS, 128), BF),
        V((NZ, MAIN_ROWS, 128), BF),
        V((NZ, NY, 16, 128), BF),
        V((NZ, NY, 16, 128), BF),
        V((NY, 16, 128), BF),
        V((NY, 16, 128), BF),
        V((2, PROJ_ROWS, 128), F32),
        V((PROJ_ROWS, 128), F32),
        V((NX, NC, 16, 128), BF),
        V((NS, NC, 16, 128), BF),
        V((NS * 16, 128), F32),
        V((6, 16, 128), F32),
        V((NC, 16, 640), BF),
        V((TURNS, NY, NC, 16, 640), BF),
        V((NY, NC, 16, 128), BF),
        V((TURNS, NY, NC, 16, 128), BF),
        V((TURNS, NX, 2, 16, BLOCK), BF),
        V((TURNS, NX, 2, 16, BLOCK), BF),
        V((TURNS, NX, 16, BLOCK), BF),
        V((TURNS, NY, NC, 16, MAIN), BF),
        V((TURNS, NY, NC, 16, MAIN), BF),
        V((TURNS, NC, 16, MAIN), BF),
        V((NZ, 16, MAIN), BF),
        V((TURNS, NC, NY, 16, 128), BF),
        V((NZ, NY, 16, 128), BF),
        V((NY, 16, 128), BF),
        V((NY, 16, 128), BF),
        dma((4,)),
        dma((1 + NZ,)),
        dma((1 + NZ,)),
        dma((1 + NZ,)),
        dma((1 + NZ,)),
        dma((1 + NZ,)),
        dma((1 + NZ,)),
        dma((1 + NZ,)),
        dma((1 + NZ,)),
        dma((1 + NZ,)),
        dma((2,)),
        dma((2,)),
        dma((1 + TURNS,)),
        dma((1 + TURNS,)),
        dma((2,)),
        dma((1 + TURNS,)),
        dma((1 + TURNS,)),
        dma((1 + TURNS,)),
        dma((1 + TURNS,)),
        dma((1 + NZ,)),
        dma((1 + NZ,)),
        dma((2,)),
    ]
    outs = pl.pallas_call(
        body,
        out_shape=(
            jax.ShapeDtypeStruct((2, D), BF),
            jax.ShapeDtypeStruct((16, BLOCK), BF),
        ),
        in_specs=[hbm] * 13,
        out_specs=(hbm, hbm),
        scratch_shapes=scratch,
        compiler_params=pltpu.CompilerParams(
            collective_id=0, has_side_effects=True, vmem_limit_bytes=56 << 20
        ),
        name="layer",
    )(
        queries,
        fresh_key_value,
        residual,
        attn_gain,
        ffn_gain,
        suffix_len,
        sample_prompt,
        prompt_key_value,
        suffix_key_value,
        out_weight,
        gate_weight,
        up_weight,
        down_weight,
    )
    return pl.pallas_call(
        hand_over,
        out_shape=tuple(jax.ShapeDtypeStruct(v.shape, v.dtype) for v in outs),
        in_specs=[vmem, vmem],
        out_specs=(vmem, vmem),
        name="hand_over",
    )(*outs)


def hand_over(mid, out, mid_to, out_to):
    mid_to[...] = mid[...]
    out_to[...] = out[...]


def solution(mesh):
    return jax.shard_map(
        local,
        mesh=mesh,
        in_specs=(
            P(("prefix", "sample"), None),
            P(("prefix", "sample"), None),
            P(("prefix", "sample"), None, None),
            P("sample", None, "prefix", None),
            P(("prefix", "sample"), None, None, None),
            P(("prefix", "sample")),
            P(),
            P("prefix", None),
            P(),
            P(),
            P("sample", "prefix"),
            P("sample", "prefix"),
            P("prefix", "sample"),
        ),
        out_specs=(P(("prefix", "sample"), None), P("prefix", "sample")),
        check_vma=False,
    )
```

```python
import functools

import jax
import jax.numpy as jnp
from jax import lax
from jax.experimental import pallas as pl
from jax.experimental.pallas import tpu as pltpu
from jax.sharding import PartitionSpec as P

MESH = pl.DeviceIdType.MESH
SCALE = 168.0 ** (-0.5)
NEGATIVE = -1e30
EPSILON = 1e-06
BF = jnp.bfloat16
F32 = jnp.float32

NZ, NY, NX, NC = 8, 4, 4, 2
NP, NS = NZ * NY, NX * NC
HEADS, KV, WIDTH = 32, 16, 128
D = 5376
CHUNKS = D // 128
PROJ_ROWS = 88
MAIN_ROWS = 72
MAIN = 544
BLOCK = 672
SUF = 192
SUFX = 208
Y_OFFSETS = X_OFFSETS = (1, 3, 2)
LAG = 6
NEAR = (0, 1, 7, 2, 6, 3, 5, 4)
FFN_ORDER = (0, 1, 4, 7, 2, 6, 5, 3)
FAR = (4, 5, 3, 6, 2, 7, 1, 0)
TURNS = 4
SCHEDULE = (
    ("a", 0), ("a", 1), ("a", 2), ("a", 3),
    ("c", 0), ("c", 1), ("c", 2), ("c", 3),
    ("e", 0), ("e", 1), ("e", 2), ("e", 3),
    ("f", 0), ("f", 1), ("f", 2), ("f", 3),
)


def dot(a, b):
    return jnp.dot(a, b, preferred_element_type=F32)


def dot_t(a, b):
    return lax.dot_general(a, b, (((1,), (1,)), ((), ())), preferred_element_type=F32)


def remote(src, dst, send_sem, recv_sem, device):
    return pltpu.make_async_remote_copy(
        src_ref=src,
        dst_ref=dst,
        send_sem=send_sem,
        recv_sem=recv_sem,
        device_id=device,
        device_id_type=MESH,
    )


def need(loads, n):
    loads[n].wait()


def body(*refs):
    ending, loads = [], []
    layer(ending, loads, *refs)
    for wait in ending:
        wait()


def layer(
    ending,
    loads,
    q_hbm,
    fresh_hbm,
    resid_hbm,
    again_hbm,
    fgain_hbm,
    slen_hbm,
    sprompt_hbm,
    pkv_hbm,
    skv_hbm,
    wout_hbm,
    wg_hbm,
    wu_hbm,
    wd_hbm,
    mid_hbm,
    out_hbm,
    q_ref,
    fresh_ref,
    resid_ref,
    again_ref,
    fgain_ref,
    slen_ref,
    sprompt_ref,
    mid_ref,
    out_ref,
    out_sem,
    pkv,
    skv,
    wout,
    ffw,
    load_sem,
    q32,
    qall,
    qflat,
    sel,
    ssuf,
    msufx,
    lsufx,
    osufx,
    osend,
    orecv,
    stsend,
    strecv,
    ozsend,
    ozrecv,
    stzsend,
    stzrecv,
    pf,
    psend,
    precv,
    pzsend,
    pzrecv,
    pbsend,
    pbrecv,
    pby,
    pbyrecv,
    gains,
    resid,
    e1send,
    e1recv,
    e1f,
    xf,
    xown,
    xall,
    xby,
    xallb,
    gu,
    gurecv,
    hid,
    ysend,
    yrecv,
    zsend,
    zrecv,
    ybsend,
    zbrecv,
    yby,
    ybyrecv,
    w_c,
    aq_z,
    aq_y,
    c_o,
    c_st,
    c_oz,
    c_stz,
    d_y,
    d_z,
    d_bz,
    d_by,
    e_1,
    e_z,
    e_y,
    e_by,
    e_bz,
    f_x,
    f_hx,
    g_y,
    g_z,
    g_bz,
    g_by,
):
    me = lax.axis_index("prefix")
    spos = lax.axis_index("sample")
    z, y = me // NY, me % NY
    x, c = spos // NC, spos % NC

    def send(src, dst, sem, recv, device):
        remote(src, dst, sem.at[0], sem.at[recv], device).start()

    def all_left(ref, sem):
        ending.append(remote(ref, ref, sem.at[0], sem.at[0], at_xc(x, c)).wait_send)

    def landed(ref, sem, recv):
        remote(ref, ref, sem.at[0], sem.at[recv], at_xc(x, c)).wait_recv()

    def at_zy(zz, yy):
        return {"prefix": zz * NY + yy, "sample": spos}

    def at_zyc(zz, yy, cc):
        return {"prefix": zz * NY + yy, "sample": x * NC + cc}

    def at_sample(s):
        return {"prefix": me, "sample": s}

    def at_xc(xx, cc):
        return {"prefix": me, "sample": xx * NC + cc}

    barrier = pltpu.get_barrier_semaphore()

    for i in range(1, NZ):
        for cc in range(NC):
            there = at_zyc(lax.rem(z + i, NZ), y, cc)
            pl.semaphore_signal(barrier, 1, device_id=there, device_id_type=MESH)
    for i in range(1, NY):
        pl.semaphore_signal(
            barrier, 1, device_id=at_zy(z, lax.rem(y + i, NY)), device_id_type=MESH
        )

    @pl.loop(1, NS)
    def _(i):
        pl.semaphore_signal(
            barrier, 1, device_id=at_sample(lax.rem(spos + i, NS)), device_id_type=MESH
        )

    def load(src, dst):
        cp = pltpu.make_async_copy(src, dst, load_sem.at[len(loads)])
        cp.start()
        loads.append(cp)

    load(q_hbm, q_ref)
    load(sprompt_hbm, sprompt_ref)
    load(slen_hbm, slen_ref)
    load(fresh_hbm, fresh_ref)
    load(resid_hbm, resid_ref)
    load(again_hbm, again_ref)
    load(fgain_hbm, fgain_ref)
    for t in range(2):
        for s in range(2):
            load(skv_hbm.at[s, t], skv.at[s, t, pl.ds(0, SUF)])
    load(pkv_hbm, pkv)

    need(loads, 0)
    for h in range(HEADS):
        q32[2 * h : 2 * h + 2, :] = q_ref[:, h * 128 : (h + 1) * 128].astype(F32)
    qall[0, 0] = q32[...].astype(BF)

    pl.semaphore_wait(barrier, NC * (NZ - 1) + NY - 1 + NS - 1)

    def spread(order, buf, sem_z, sem_y):
        def to_y(n):
            for i in Y_OFFSETS:
                there = at_zy(z, lax.rem(y + i, NY))
                send(buf.at[n, 0], buf.at[n, (-i) % NY], sem_y, 1 + n, there)

        def start():
            for n in range(NZ - 1, 0, -1):
                slot = order.index((-order[n]) % NZ)
                there = at_zy(lax.rem(z + order[n], NZ), y)
                send(buf.at[0, 0], buf.at[slot, 0], sem_z, 1 + slot, there)
            to_y(0)
            all_left(buf.at[pl.ds(1, NZ - 1), 0], sem_z)
            all_left(buf.at[pl.ds(0, NZ), pl.ds(1, NY - 1)], sem_y)

        def pass_on(n):
            landed(buf.at[n, 0], sem_z, 1 + n)
            to_y(n)

        def take(n):
            landed(buf.at[n, pl.ds(1, NY - 1)], sem_y, 1 + n)

        return start, pass_on, take

    q_start, q_pass, q_take = spread(NEAR, qall, aq_z, aq_y)
    q_start()

    need(loads, 1)
    @pl.loop(0, 2 * NP)
    def _(r):
        value = sprompt_ref[lax.rem(r, NP) * 16 + 2 * spos + r // NP] - 2 * spos
        row = jnp.full((1, 128), value, jnp.int32).astype(F32)
        sel[pl.ds(r, 1), :] = row
        sel[pl.ds(r + 2 * NP, 1), :] = row

    msufx[...] = jnp.full(msufx.shape, NEGATIVE, F32)
    q_pass(1)

    need(loads, 3)
    first_row = lax.broadcasted_iota(jnp.int32, (16, 2048), 0) == 0
    for s in range(2):
        for t in range(2):
            row = jnp.broadcast_to(fresh_ref[s, t : t + 1, :].astype(F32), (16, 2048))
            skv[s, t, SUF:SUFX, :] = jnp.where(first_row, row, 0.0).astype(BF)
    q_pass(2)
    for s in range(2):
        need(loads, 7 + s)

    def suffix_scores(k):
        lanes = slice(k * 128, (k + 1) * 128)
        rows = q32[4 * k : 4 * k + 4, :].astype(BF)
        odd = lax.broadcasted_iota(jnp.int32, (4, SUFX), 0) % 2 == 1
        ssuf[4 * k : 4 * k + 4, :] = jnp.where(
            odd, dot_t(rows, skv[1, 0, :, lanes]), dot_t(rows, skv[0, 0, :, lanes])
        )

    for k in range(KV // 2):
        suffix_scores(k)
    q_pass(3)
    for k in range(KV // 2, KV):
        suffix_scores(k)
    q_pass(4)
    odd = lax.broadcasted_iota(jnp.int32, (64, SUFX), 0) % 2 == 1
    slot = lax.broadcasted_iota(jnp.int32, (64, SUFX), 1)
    need(loads, 2)
    length = jnp.where(odd, slen_ref[1], slen_ref[0])
    scores = jnp.where((slot < length) | (slot == SUF), ssuf[...] * SCALE, NEGATIVE)
    msuf = jnp.max(scores, axis=1, keepdims=True)
    expo = jnp.exp(scores - msuf)
    lsuf = jnp.broadcast_to(jnp.sum(expo, axis=1, keepdims=True), (64, 128))
    msuf = jnp.broadcast_to(msuf, (64, 128))
    even_w = jnp.where(odd, 0.0, expo)
    odd_w = jnp.where(odd, expo, 0.0)
    q_pass(5)
    q_pass(6)
    q_pass(7)
    lsufx[...] = jnp.zeros(lsufx.shape, F32)
    osufx[...] = jnp.zeros(osufx.shape, F32)
    for s in range(2):
        need(loads, 9 + s)
    for k in range(KV):
        lanes = slice(k * 128, (k + 1) * 128)
        part = slice(4 * k, 4 * k + 4)
        o = dot(even_w[part].astype(BF), skv[0, 1, :, lanes]) + dot(
            odd_w[part].astype(BF), skv[1, 1, :, lanes]
        )
        for g in range(2):
            for s in range(2):
                src = 4 * k + 2 * g + s
                dst = k * 128 + g * 64 + s * 32 + me
                msufx[pl.ds(dst, 1), :] = msuf[src : src + 1]
                lsufx[pl.ds(dst, 1), :] = lsuf[src : src + 1]
                osufx[pl.ds(dst, 1), :] = o[2 * g + s : 2 * g + s + 1]

    for n in range(NZ):
        q_take(n)
        for i in range(NY):
            owner = lax.rem(z + NEAR[n], NZ) * NY + lax.rem(y + i, NY)
            qflat[pl.ds(pl.multiple_of(owner * 64, 64), 64), :] = qall[n, i].astype(F32)

    load(wout_hbm, wout)
    for t, ref in enumerate((wg_hbm, wu_hbm, wd_hbm)):
        load(ref, ffw.at[t, c])
        send(ref, ffw.at[t, c], w_c, 1 + t, at_xc(x, 1 - c))
    all_left(ffw.at[pl.ds(0, 3), 0], w_c)

    need(loads, 11)
    chosen = sel[...] > 0.5
    lane = lax.broadcasted_iota(jnp.int32, (128, 128), 1)
    diagonal = lax.broadcasted_iota(jnp.int32, (64, 64), 0) == lax.broadcasted_iota(
        jnp.int32, (64, 64), 1
    )

    def attend(k):
        lanes = pl.ds(pl.multiple_of(k * 128, 128), 128)
        rows = pl.ds(pl.multiple_of(k * 128, 128), 128)
        q = jnp.concatenate(
            [qflat[pl.ds(4 * k + t, 32, stride=64), :] for t in range(4)], axis=0
        ).astype(BF)
        scores = jnp.where(chosen, dot_t(q, pkv[1, 0, :, lanes]), dot_t(q, pkv[0, 0, :, lanes]))
        scores = scores * SCALE
        ms = msufx[rows, :]
        m = jnp.maximum(ms, jnp.max(scores, axis=1, keepdims=True))
        expo = jnp.exp(scores - m)
        a = jnp.exp(ms - m)
        total = jnp.sum(expo, axis=1, keepdims=True) + a * lsufx[rows, :]
        w0 = jnp.where(chosen, 0.0, expo).astype(BF)
        w1 = jnp.where(chosen, expo, 0.0).astype(BF)
        o = dot(w0, pkv[0, 1, :, lanes]) + dot(w1, pkv[1, 1, :, lanes]) + a * osufx[rows, :]
        return o.astype(BF), m, total

    def o_to_y(n, i):
        yy = lax.rem(y + i, NY)
        send(osend.at[n, yy], orecv.at[n, (-i) % NY], c_o, 1 + n, at_zy(z, yy))
        send(stsend.at[n], strecv.at[n, (-i) % NY], c_st, 1 + n, at_zy(z, yy))

    def blend(weights, parts):
        total = None
        for low in (False, True):
            pieces = []
            for w in weights:
                w = w[:, :64]
                high = w.astype(BF).astype(F32)
                w = w - high if low else high
                pieces.append(jnp.where(diagonal, jnp.broadcast_to(w, (64, 64)), 0.0).astype(BF))
            term = dot(jnp.concatenate(pieces, axis=1), jnp.concatenate(parts, axis=0))
            total = term if total is None else total + term
        return total

    odd_y = jnp.zeros((1, 128), jnp.int32) + lax.rem(y, 2) == 1
    stat_row = 2 * (y // 2)

    def merge(n):
        maxima, totals, parts = [], [], []
        landed(orecv.at[n, pl.ds(1, NY - 1)], c_o, 1 + n)
        landed(strecv.at[n, pl.ds(1, NY - 1)], c_st, 1 + n)
        for i in range(NY):
            if i:
                parts.append(orecv[n, i])
                m = strecv[n, i, pl.ds(stat_row, 1), :]
                total = strecv[n, i, pl.ds(stat_row + 1, 1), :]
            else:
                parts.append(osend[n, y])
                m = stsend[n, pl.ds(stat_row, 1), :]
                total = stsend[n, pl.ds(stat_row + 1, 1), :]
            maxima.append(jnp.where(odd_y, pltpu.roll(m, 64, 1), m))
            totals.append(jnp.where(odd_y, pltpu.roll(total, 64, 1), total))
        top = functools.reduce(jnp.maximum, maxima)
        weights = [jnp.exp(m - top) for m in maxima]
        total = sum(w * t for w, t in zip(weights, totals))
        ozsend[n] = blend(weights, parts).astype(BF)
        first = lax.broadcasted_iota(jnp.int32, (8, 128), 0) == 0
        stzsend[n] = jnp.where(
            first, jnp.broadcast_to(top, (8, 128)), jnp.broadcast_to(total, (8, 128))
        )
        if FAR[n]:
            there = at_zy(lax.rem(z + FAR[n], NZ), y)
            send(ozsend.at[n], ozrecv.at[n], c_oz, 1 + n, there)
            send(stzsend.at[n], stzrecv.at[n], c_stz, 1 + n, there)

    for n in range(NZ):
        zz = lax.rem(z + FAR[n], NZ)
        o0, m0, t0 = attend(2 * zz)
        o1, m1, t1 = attend(2 * zz + 1)
        for g in range(2):
            osend[n, g] = o0[g * 64 : (g + 1) * 64]
            osend[n, 2 + g] = o1[g * 64 : (g + 1) * 64]
        stats = jnp.where(
            lane == 0, m0, jnp.where(lane == 1, t0, jnp.where(lane == 2, m1, t1))
        )
        stsend[n] = stats.T[0:8]
        for i in Y_OFFSETS:
            o_to_y(n, i)
        if n >= LAG:
            merge(n - LAG)
    for n in range(NZ - LAG, NZ):
        merge(n)

    all_left(orecv.at[pl.ds(0, NZ), pl.ds(1, NY - 1)], c_o)
    all_left(strecv.at[pl.ds(0, NZ), pl.ds(1, NY - 1)], c_st)
    all_left(ozrecv.at[pl.ds(0, NZ - 1)], c_oz)
    all_left(stzrecv.at[pl.ds(0, NZ - 1)], c_stz)

    maxima, totals, parts = [], [], []
    for n in range(NZ - 1):
        landed(ozrecv.at[n], c_oz, 1 + n)
        landed(stzrecv.at[n], c_stz, 1 + n)
        maxima.append(stzrecv[n, 0:1, :])
        totals.append(stzrecv[n, 1:2, :])
        parts.append(ozrecv[n])
    maxima.append(stzsend[NZ - 1, 0:1, :])
    totals.append(stzsend[NZ - 1, 1:2, :])
    parts.append(ozsend[NZ - 1])
    top = functools.reduce(jnp.maximum, maxima)
    weights = [jnp.exp(m - top) for m in maxima]
    total = sum(w * t for w, t in zip(weights, totals))
    attended = blend([w / total for w in weights], parts).astype(BF)

    need(loads, 12)
    for j in range(CHUNKS // 2):
        r = dot(attended, wout[:, 256 * j : 256 * (j + 1)])
        for t in range(2):
            for s in range(2):
                pf[pl.ds(4 * j + 2 * t + s, NP, stride=PROJ_ROWS), :] = r[
                    s * 32 : (s + 1) * 32, t * 128 : (t + 1) * 128
                ]
    for s in range(2 * CHUNKS, PROJ_ROWS):
        pf[pl.ds(s, NP, stride=PROJ_ROWS), :] = jnp.zeros((NP, 128), F32)

    def reduced(n_z, y_out, y_in, z_out, z_in, sem_y, sem_z):
        def to_y(n, i):
            there = at_zy(z, lax.rem(y + i, NY))
            send(y_out.at[n, i], y_in.at[n, (-i) % NY], sem_y, 1 + n, there)

        def add_y(n):
            landed(y_in.at[n, pl.ds(1, NY - 1)], sem_y, 1 + n)
            total = y_out[n, 0].astype(F32)
            for i in Y_OFFSETS:
                total = total + y_in[n, i].astype(F32)
            return total

        def to_z(n, total):
            z_out[n] = total.astype(BF)
            there = at_zy(lax.rem(z + n_z[n], NZ), y)
            send(z_out.at[n], z_in.at[n], sem_z, 1 + n, there)

        def add_z(n):
            landed(z_in.at[n], sem_z, 1 + n)
            return z_in[n].astype(F32)

        all_left(y_in.at[pl.ds(0, NZ), pl.ds(1, NY - 1)], sem_y)
        all_left(z_in.at[pl.ds(0, NZ - 1)], sem_z)
        return to_y, add_y, to_z, add_z

    p_to_y, p_add_y, p_to_z, p_add_z = reduced(FAR, psend, precv, pzsend, pzrecv, d_y, d_z)
    for n in range(NZ):
        for i in Y_OFFSETS + (0,):
            o = lax.rem(z + FAR[n], NZ) * NY + lax.rem(y + i, NY)
            start = pl.multiple_of(o * PROJ_ROWS, 8)
            start_b = pl.multiple_of(o * PROJ_ROWS + MAIN_ROWS, 8)
            psend[n, i] = pf[pl.ds(start, MAIN_ROWS), :].astype(BF)
            pbsend[n, i] = pf[pl.ds(start_b, PROJ_ROWS - MAIN_ROWS), :].astype(BF)
            if i:
                p_to_y(n, i)
        if FAR[n]:
            there = at_zy(lax.rem(z + FAR[n], NZ), y)
            send(pbsend.at[n], pbrecv.at[n], d_bz, 1 + n, there)
    all_left(pbrecv.at[pl.ds(0, NZ - 1)], d_bz)
    for n in (4, 5, 6):
        need(loads, n)
    for j in range(CHUNKS):
        cols = slice(j * 128, (j + 1) * 128)
        resid[2 * j : 2 * j + 2, :] = resid_ref[:, cols].astype(F32)
        gains[0, 2 * j : 2 * j + 2, :] = jnp.broadcast_to(again_ref[cols].reshape(1, 128), (2, 128))
        gains[1, 2 * j : 2 * j + 2, :] = jnp.broadcast_to(fgain_ref[cols].reshape(1, 128), (2, 128))
    for n in range(NZ - 1):
        p_to_z(n, p_add_y(n))
    rest = pbsend[NZ - 1].astype(F32)
    for n in range(NZ - 1):
        landed(pbrecv.at[n], d_bz, 1 + n)
        rest = rest + pbrecv[n].astype(F32)
    pby[...] = rest.astype(BF)
    for i in Y_OFFSETS:
        send(pby.at[i], pbyrecv.at[(-i) % NY], d_by, 1, at_zy(z, lax.rem(y + i, NY)))
    all_left(pbyrecv.at[pl.ds(1, NY - 1)], d_by)
    projected = p_add_y(NZ - 1)
    for n in range(NZ - 1):
        projected = projected + p_add_z(n)
    landed(pbyrecv.at[pl.ds(1, NY - 1)], d_by, 1)
    rest = pby[0].astype(F32)
    for i in Y_OFFSETS:
        rest = rest + pbyrecv[i].astype(F32)
    projected = jnp.concatenate([projected, rest], axis=0)

    row = lax.broadcasted_iota(jnp.int32, (PROJ_ROWS, 128), 0)
    odd = row % 2 == 1
    real = row < 2 * CHUNKS

    def normed(values, gain):
        square = jnp.where(real, values * values, 0.0)
        second = jnp.sum(jnp.where(odd, square, 0.0))
        first = jnp.sum(jnp.where(odd, 0.0, square))
        inv = jnp.where(odd, second, first) * (1.0 / D) + EPSILON
        return values * lax.rsqrt(inv) * gain

    midway = (resid[...] + normed(projected, gains[0])).astype(BF)
    settled = midway.astype(F32)
    ffn_in = normed(settled, gains[1]).astype(BF).astype(F32)
    ffn_in = jnp.where(real, ffn_in, 0.0)

    lane = lax.broadcasted_iota(jnp.int32, (12, 128), 1)
    rolled = [ffn_in if o == 0 else pltpu.roll(ffn_in, 128 - o, 1) for o in (0, 32, 64, 96)]
    for b in range(NS):
        o, j0 = 32 * (b % 4), (21 * b) // 4
        v = rolled[b % 4]
        piece = v[2 * j0 : 2 * j0 + 12]
        if o:
            piece = jnp.where(lane < 128 - o, piece, v[2 * j0 + 2 : 2 * j0 + 14])
        piece = jnp.concatenate([piece, jnp.zeros((4, 128), F32)], axis=0)
        e1send[b // NC, b % NC] = piece.astype(BF)

    for i in range(1, NS):
        b = lax.rem(spos + i, NS)
        send(e1send.at[b // NC], e1recv.at[spos], e_1, 1, at_sample(b))
    all_left(e1recv.at[pl.ds(1, NS - 1)], e_1)
    e1recv[spos] = e1send[x]
    for j in range(CHUNKS):
        mid_ref[:, j * 128 : (j + 1) * 128] = settled[2 * j : 2 * j + 2].astype(BF)
    mid_copy = pltpu.make_async_copy(mid_ref, mid_hbm, out_sem.at[0])
    mid_copy.start()
    ending.append(mid_copy.wait)
    landed(e1recv.at[pl.ds(1, NS - 1)], e_1, 1)
    for cc in range(NC):
        for b in range(NS):
            e1f[16 * b : 16 * (b + 1), :] = e1recv[b, cc].astype(F32)
        for i in range(6):
            for s in range(2):
                xf[i, pl.ds(s, 8, stride=2), :] = e1f[pl.ds(2 * i + s, 8, stride=16), :]
        xby[0, cc] = xf[0, 0:16].astype(BF)
        for i in range(1, 6):
            xown[cc, :, (i - 1) * 128 : i * 128] = xf[i, 0:16].astype(BF)

    def turn(t):
        return FFN_ORDER[2 * t] * (1 - c) + FFN_ORDER[2 * t + 1] * c

    def x_to_z(t):
        send(xown, xall.at[t, 0], e_z, 1 + t, at_zy(lax.rem(z + NZ - turn(t), NZ), y))

    def x_to_y(t):
        for i in Y_OFFSETS:
            there = at_zy(z, lax.rem(y + i, NY))
            send(xall.at[t, 0], xall.at[t, (-i) % NY], e_y, 1 + t, there)

    for i in Y_OFFSETS:
        send(xby.at[0], xby.at[(-i) % NY], e_by, 1, at_zy(z, lax.rem(y + i, NY)))
    all_left(xby.at[pl.ds(1, NY - 1)], e_by)

    def xb_to_z(t):
        send(xby, xallb.at[t], e_bz, 1 + t, at_zy(lax.rem(z + NZ - turn(t), NZ), y))

    for t in (3, 2, 1):
        x_to_z(t)

    @pl.when(c == 0)
    def _():
        xall[0, 0] = xown[...]

    @pl.when(c == 1)
    def _():
        x_to_z(0)
        landed(xall.at[0, 0], e_z, 1)

    x_to_y(0)
    landed(xby.at[pl.ds(1, NY - 1)], e_by, 1)
    for t in (3, 2, 1):
        xb_to_z(t)

    @pl.when(c == 0)
    def _():
        xallb[0] = xby[...]

    @pl.when(c == 1)
    def _():
        xb_to_z(0)

    for t in range(1, TURNS):
        landed(xall.at[t, 0], e_z, 1 + t)
        x_to_y(t)
    all_left(xall.at[pl.ds(0, TURNS), pl.ds(1, NY - 1)], e_y)

    def some_left(ref, sem):
        less = ref.at[pl.ds(1, ref.shape[0] - 1)]
        for cc, sent in ((0, less), (1, ref)):

            @pl.when(c == cc)
            def _(sent=sent):
                remote(sent, sent, sem.at[0], sem.at[0], at_xc(x, c)).wait_send()

    ending.append(lambda: some_left(xall.at[pl.ds(0, TURNS), 0], e_z))
    ending.append(lambda: some_left(xallb, e_bz))

    for t in range(3):
        need(loads, 13 + t)
        landed(ffw.at[t, 1 - c], w_c, 1 + t)

    def stage_a(t):
        landed(xall.at[t, pl.ds(1, NY - 1)], e_y, 1 + t)
        if t:
            landed(xallb.at[t], e_bz, 1 + t)
        else:

            @pl.when(c == 1)
            def _():
                landed(xallb.at[0], e_bz, 1)

        v = []
        for cc in range(NC):
            main = xall[t, :, cc].reshape(64, 640)[:, :MAIN]
            v.append(jnp.concatenate([xallb[t, :, cc].reshape(64, 128), main], axis=1))
        for n in range(2):
            part = dot(v[0], ffw[n, 0]) + dot(v[1], ffw[n, 1])
            gu[t, :, n] = part.astype(BF).reshape(NY, 16, BLOCK)
        for i in X_OFFSETS:
            xx = lax.rem(x + i, NX)
            send(gu.at[t, xx], gurecv.at[t, i], f_x, 1 + t, at_xc(xx, c))

    def stage_c(t):
        landed(gurecv.at[t, pl.ds(1, NX - 1)], f_x, 1 + t)
        total = gu[t, x].astype(F32)
        for i in X_OFFSETS:
            total = total + gurecv[t, i].astype(F32)
        own = hid.at[t, x]
        own[...] = (jax.nn.gelu(total[0], approximate=True) * total[1]).astype(BF)
        for i in X_OFFSETS:
            send(own, own, f_hx, 1 + t, at_xc(lax.rem(x + i, NX), c))

    def stage_e(t):
        landed(hid.at[t, pl.ds(0, NX - 1)], f_hx, 1 + t)
        hidden = hid[t].reshape(64, BLOCK)
        for cc in range(NC):
            down = dot(hidden, ffw[2, cc]).astype(BF)
            ybsend[t, cc] = down[:, :128].reshape(NY, 16, 128)
            ysend[t, :, cc] = down[:, 128:].reshape(NY, 16, MAIN)
        for i in Y_OFFSETS:
            there = at_zy(z, lax.rem(y + i, NY))
            send(ysend.at[t, i], yrecv.at[t, (-i) % NY], g_y, 1 + t, there)
        to_cores(t, lambda n, cc, there: send(ybsend.at[t, cc], zbrecv.at[n], g_bz, 1 + n, there))

    def to_cores(t, send_one):
        zz = lax.rem(z + turn(t), NZ)
        n = 2 * t + c
        send_one(n, 1, at_zyc(zz, y, 1))
        if t:
            send_one(n, 0, at_zyc(zz, y, 0))
        else:

            @pl.when(c == 1)
            def _():
                send_one(n, 0, at_zyc(zz, y, 0))

    def stage_f(t):
        landed(yrecv.at[t, pl.ds(1, NY - 1)], g_y, 1 + t)
        total = ysend[t, 0].astype(F32)
        for i in Y_OFFSETS:
            total = total + yrecv[t, i].astype(F32)
        zsend[t] = total.astype(BF)
        to_cores(t, lambda n, cc, there: send(zsend.at[t, cc], zrecv.at[n], g_z, 1 + n, there))

    all_left(gurecv.at[pl.ds(0, TURNS), pl.ds(1, NX - 1)], f_x)
    all_left(hid.at[pl.ds(0, TURNS), pl.ds(0, NX - 1)], f_hx)
    all_left(yrecv.at[pl.ds(0, TURNS), pl.ds(1, NY - 1)], g_y)
    stages = {"a": stage_a, "c": stage_c, "e": stage_e, "f": stage_f}
    for name, t in SCHEDULE:
        stages[name](t)

    def over_z(recv, own, sem):
        @pl.when(c == 0)
        def _():
            recv[0] = own[...]

        @pl.when(c == 1)
        def _():
            landed(recv.at[0], sem, 1)

        total = recv[0].astype(F32)
        for n in range(1, NZ):
            landed(recv.at[n], sem, 1 + n)
            total = total + recv[n].astype(F32)
        ending.append(lambda: some_left(recv, sem))
        return total

    yby[...] = over_z(zbrecv, ybsend.at[0, 0], g_bz).astype(BF)
    for i in Y_OFFSETS:
        send(yby.at[i], ybyrecv.at[(-i) % NY], g_by, 1, at_zy(z, lax.rem(y + i, NY)))
    all_left(ybyrecv.at[pl.ds(1, NY - 1)], g_by)
    out_ref[:, 128:] = over_z(zrecv, zsend.at[0, 0], g_z).astype(BF)
    landed(ybyrecv.at[pl.ds(1, NY - 1)], g_by, 1)
    rest = yby[0].astype(F32)
    for i in Y_OFFSETS:
        rest = rest + ybyrecv[i].astype(F32)
    out_ref[:, :128] = rest.astype(BF)
    out_copy = pltpu.make_async_copy(out_ref, out_hbm, out_sem.at[1])
    out_copy.start()
    ending.append(out_copy.wait)


def local(
    residual,
    queries,
    fresh_key_value,
    prompt_key_value,
    suffix_key_value,
    suffix_len,
    sample_prompt,
    out_weight,
    attn_gain,
    ffn_gain,
    gate_weight,
    up_weight,
    down_weight,
):
    hbm = pl.BlockSpec(memory_space=pl.ANY)
    vmem = pl.BlockSpec(memory_space=pltpu.VMEM)
    V = pltpu.VMEM
    dma = pltpu.SemaphoreType.DMA
    scratch = [
        V((2, HEADS * WIDTH), BF),
        V((2, 2, KV * WIDTH), BF),
        V((2, D), BF),
        V((D,), F32),
        V((D,), F32),
        pltpu.SMEM((2,), jnp.int32),
        pltpu.SMEM((2 * NP * NS,), jnp.int32),
        V((2, D), BF),
        V((16, BLOCK), BF),
        dma((2,)),
        V((2, 2, 128, 2048), BF),
        V((2, 2, SUFX, 2048), BF),
        V((128, D), BF),
        V((3, NC, BLOCK, BLOCK), BF),
        dma((16,)),
        V((64, 128), F32),
        V((NZ, NY, 64, 128), BF),
        V((NP * 64 + 64, 128), F32),
        V((128, 128), F32),
        V((64, SUFX), F32),
        V((KV * 128, 128), F32),
        V((KV * 128, 128), F32),
        V((KV * 128, 128), F32),
        V((NZ, NY, 64, 128), BF),
        V((NZ, NY, 64, 128), BF),
        V((NZ, 8, 128), F32),
        V((NZ, NY, 8, 128), F32),
        V((NZ, 64, 128), BF),
        V((NZ, 64, 128), BF),
        V((NZ, 8, 128), F32),
        V((NZ, 8, 128), F32),
        V((NP * PROJ_ROWS + PROJ_ROWS, 128), F32),
        V((NZ, NY, MAIN_ROWS, 128), BF),
        V((NZ, NY, MAIN_ROWS, 128), BF),
        V((NZ, MAIN_ROWS, 128), BF),
        V((NZ, MAIN_ROWS, 128), BF),
        V((NZ, NY, 16, 128), BF),
        V((NZ, NY, 16, 128), BF),
        V((NY, 16, 128), BF),
        V((NY, 16, 128), BF),
        V((2, PROJ_ROWS, 128), F32),
        V((PROJ_ROWS, 128), F32),
        V((NX, NC, 16, 128), BF),
        V((NS, NC, 16, 128), BF),
        V((NS * 16 + 16, 128), F32),
        V((6, 24, 128), F32),
        V((NC, 16, 640), BF),
        V((TURNS, NY, NC, 16, 640), BF),
        V((NY, NC, 16, 128), BF),
        V((TURNS, NY, NC, 16, 128), BF),
        V((TURNS, NX, 2, 16, BLOCK), BF),
        V((TURNS, NX, 2, 16, BLOCK), BF),
        V((TURNS, NX, 16, BLOCK), BF),
        V((TURNS, NY, NC, 16, MAIN), BF),
        V((TURNS, NY, NC, 16, MAIN), BF),
        V((TURNS, NC, 16, MAIN), BF),
        V((NZ, 16, MAIN), BF),
        V((TURNS, NC, NY, 16, 128), BF),
        V((NZ, NY, 16, 128), BF),
        V((NY, 16, 128), BF),
        V((NY, 16, 128), BF),
        dma((4,)),
        dma((1 + NZ,)),
        dma((1 + NZ,)),
        dma((1 + NZ,)),
        dma((1 + NZ,)),
        dma((1 + NZ,)),
        dma((1 + NZ,)),
        dma((1 + NZ,)),
        dma((1 + NZ,)),
        dma((1 + NZ,)),
        dma((2,)),
        dma((2,)),
        dma((1 + TURNS,)),
        dma((1 + TURNS,)),
        dma((2,)),
        dma((1 + TURNS,)),
        dma((1 + TURNS,)),
        dma((1 + TURNS,)),
        dma((1 + TURNS,)),
        dma((1 + NZ,)),
        dma((1 + NZ,)),
        dma((2,)),
    ]
    outs = pl.pallas_call(
        body,
        out_shape=(
            jax.ShapeDtypeStruct((2, D), BF),
            jax.ShapeDtypeStruct((16, BLOCK), BF),
        ),
        in_specs=[hbm] * 13,
        out_specs=(hbm, hbm),
        scratch_shapes=scratch,
        compiler_params=pltpu.CompilerParams(
            collective_id=0, has_side_effects=True, vmem_limit_bytes=56 << 20
        ),
        name="layer",
    )(
        queries,
        fresh_key_value,
        residual,
        attn_gain,
        ffn_gain,
        suffix_len,
        sample_prompt,
        prompt_key_value,
        suffix_key_value,
        out_weight,
        gate_weight,
        up_weight,
        down_weight,
    )
    return pl.pallas_call(
        hand_over,
        out_shape=tuple(jax.ShapeDtypeStruct(v.shape, v.dtype) for v in outs),
        in_specs=[vmem, vmem],
        out_specs=(vmem, vmem),
        name="hand_over",
    )(*outs)


def hand_over(mid, out, mid_to, out_to):
    mid_to[...] = mid[...]
    out_to[...] = out[...]


def solution(mesh):
    return jax.shard_map(
        local,
        mesh=mesh,
        in_specs=(
            P(("prefix", "sample"), None),
            P(("prefix", "sample"), None),
            P(("prefix", "sample"), None, None),
            P("sample", None, "prefix", None),
            P(("prefix", "sample"), None, None, None),
            P(("prefix", "sample")),
            P(),
            P("prefix", None),
            P(),
            P(),
            P("sample", "prefix"),
            P("sample", "prefix"),
            P("prefix", "sample"),
        ),
        out_specs=(P(("prefix", "sample"), None), P("prefix", "sample")),
        check_vma=False,
    )
```
